128 devices in a mesh: sx: 8 (over x, core), sy: 16 (over y, z).
Axes of the slice: x: 4, y: 4, z: 4, core: 2. Of those that a mesh axis runs over, the one named last changes fastest.
Arguments:
- weights: float32 [2, 256, 256, 256], P(None, 'sx', 'sy'), may hold values from -0.125 to 0.125
Outputs:
- target_weights: float32 [2, 256, 256, 256], P(None, 'sx', 'sy')
The draws below stay inside these ranges and needn't reach their ends.
All inputs are finite; a program needn't handle non-finite values.
Results may differ from the reference program's by a relative error of at most 0.0015.
Values sent between devices are 32-bit elements; how exact they have to be, the bound alone decides.
No kernel may reach another device: no remote copies, remote signals or barrier semaphores. Data moves between devices by JAX's collectives and lax.ppermute only.
A program may use at most 128 MiB of HBM per device.

```python
import math
import jax
import jax.numpy as jnp
import numpy as np
from jax import lax

CHEB = 8
RANK = 64
RHS = 4
GRID = 4096
LEVELS = 8
START = 2
BOXES = 256


def shard_levels(own_key, dims, cuts, least, top_value):
    gain, own = 1.0, jax.random.fold_in(own_key, 6)
    for dim, blocks in cuts:
        draws = jnp.exp(jax.random.uniform(jax.random.fold_in(own, dim), (blocks,), jnp.float32, least / len(cuts), top_value / len(cuts)))
        gain = gain * jnp.repeat(draws, dims[dim] // blocks).reshape([-1 if axis == dim else 1 for axis in range(len(dims))])
    return gain


def normal_values(stream_key, dims, scale, bound, split=(), kind=jnp.bfloat16):
    gain = shard_levels(stream_key, dims, split, -0.22, 0.18) if split else 1.0
    result = jax.random.normal(stream_key, dims, jnp.float32) * scale * gain
    return jnp.minimum(jnp.maximum(result, -bound), bound).astype(kind)


def setup_inputs(seed: int = 0) -> dict:
    keys = jax.random.split(jax.random.key(seed), 2)
    return {
        "weights": normal_values(keys[0], (2, BOXES, BOXES, RHS * RANK), (0.56 ** LEVELS), 0.125, ((1, 8), (2, 16)), jnp.float32),
    }


full_turn = 2.0 * math.pi

def lagrange_tables(node_count):
    cheb_nodes = 0.5 * np.cos((2.0 * np.arange(node_count) + 1.0) * math.pi / (2.0 * node_count))
    single = np.ones((2, node_count, node_count))
    for child_bit in range(2):
        for source in range(node_count):
            location = (child_bit - 0.5) / 2.0 + cheb_nodes[source] / 2.0
            for target in range(node_count):
                for another in range(node_count):
                    if another != target:
                        single[child_bit, source, target] *= (location - cheb_nodes[another]) / (cheb_nodes[target] - cheb_nodes[another])
    paired = single[:, None, :, None, :, None] * single[None, :, None, :, None, :]
    paired = paired.reshape(2, 2, node_count * node_count, node_count * node_count)
    return (cheb_nodes, paired)

def phase_parts(centre_one, centre_two, wave_one, wave_two):
    bending = (2.0 + jnp.sin(full_turn * centre_one)[:, None] * jnp.sin(full_turn * centre_two)[None, :]) / 16.0
    linear = (centre_one[:, None] * wave_one)[:, None, :, None] + (centre_two[:, None] * wave_two)[None, :, None, :]
    radius = jnp.sqrt(wave_one[:, None, :, None] ** 2 + wave_two[None, :, None, :] ** 2)
    phase_sum = linear + bending[:, :, None, None] * radius
    angles = full_turn * (phase_sum - jnp.floor(phase_sum))
    table_shape = (centre_one.shape[0], centre_two.shape[0], -1)
    return (jnp.cos(angles).reshape(table_shape), jnp.sin(angles).reshape(table_shape))

def box_geometry(positions, level_step):
    parent_box = jnp.zeros_like(positions)
    for bit_index in range(level_step):
        parent_box = parent_box + ((positions >> bit_index & 1) << level_step - 1 - bit_index)
    return (parent_box, positions >> level_step)

def centres(parent_box, bit_value, level):
    return (2.0 * parent_box.astype(jnp.float32) + (bit_value + 0.5)) * 0.5 ** (level + 1)

def waves(box_index, level, node_points):
    box_width = 2.0 ** level
    return (-GRID / 2.0 + (box_index.astype(jnp.float32) + 0.5) * box_width)[:, None] + box_width * node_points[None, :]

def split_view(entries, position):
    if position < 0:
        return (entries, 1, 1)
    return (entries >> position + 1, 2, 1 << position)

def group_first(values, high_part, group_part, low_part):
    return values.reshape(high_part, group_part, low_part)[:, 0, :].reshape(-1)

def mix_level(weights, rows_one, rows_two, level_step, place_one, place_two):
    node_values, paired = lagrange_tables(CHEB)
    node_points = jnp.asarray(node_values, jnp.float32)
    table = jnp.asarray(paired, jnp.float32)
    level = START + level_step
    column_count, point_count = (weights.shape[3], weights.shape[4])
    high_one, group_one, low_one = split_view(weights.shape[1], place_one)
    high_two, group_two, low_two = split_view(weights.shape[2], place_two)
    parent_one, child_one = box_geometry(rows_one, level_step)
    parent_two, child_two = box_geometry(rows_two, level_step)
    if place_one < 0:
        table = lax.dynamic_slice_in_dim(table, rows_one[0] >> level_step & 1, 1, 0)
    if place_two < 0:
        table = lax.dynamic_slice_in_dim(table, rows_two[0] >> level_step & 1, 1, 1)
    child_wave_one = waves(child_one, level, node_points)
    child_wave_two = waves(child_two, level, node_points)
    outer_one = group_first(parent_one, high_one, group_one, low_one)
    outer_two = group_first(parent_two, high_two, group_two, low_two)
    parent_wave_one = waves(group_first(child_one, high_one, group_one, low_one) >> 1, level + 1, node_points)
    parent_wave_two = waves(group_first(child_two, high_two, group_two, low_two) >> 1, level + 1, node_points)
    results = []
    for bit_one in range(2):
        row_parts = []
        for bit_two in range(2):
            cos_in, sin_in = phase_parts(centres(parent_one, bit_one, level), centres(parent_two, bit_two, level), child_wave_one, child_wave_two)
            cos_in = cos_in[:, :, None, :]
            sin_in = sin_in[:, :, None, :]
            real_part = cos_in * weights[0] + sin_in * weights[1]
            imag_part = cos_in * weights[1] - sin_in * weights[0]
            rotated = jnp.stack([real_part, imag_part]).reshape(2, high_one, group_one, low_one, high_two, group_two, low_two, column_count, point_count)
            mixture = jnp.einsum('rhclmdnkt,cdtu->rhlmnku', rotated, table, precision=lax.Precision.HIGHEST)
            cos_out, sin_out = phase_parts(centres(outer_one, bit_one, level), centres(outer_two, bit_two, level), parent_wave_one, parent_wave_two)
            cos_out = cos_out.reshape(high_one, low_one, high_two, low_two, 1, point_count)
            sin_out = sin_out.reshape(high_one, low_one, high_two, low_two, 1, point_count)
            row_parts.append(jnp.stack([cos_out * mixture[0] - sin_out * mixture[1], sin_out * mixture[0] + cos_out * mixture[1]]))
        results.append(jnp.stack(row_parts))
    return jnp.stack(results)

def place_bits(mixture, entries_one, entries_two):
    turned = jnp.transpose(mixture, (2, 3, 0, 4, 5, 1, 6, 7, 8))
    return turned.reshape(2, entries_one, entries_two, mixture.shape[-2], mixture.shape[-1])

def reference(weights):
    positions = jnp.arange(BOXES, dtype=jnp.int32)
    weights = weights.reshape(2, BOXES, BOXES, RHS, RANK)
    for level_step in range(LEVELS):
        weights = place_bits(mix_level(weights, positions, positions, level_step, level_step, level_step), BOXES, BOXES)
    return weights.reshape(2, BOXES, BOXES, RHS * RANK)
```

```python
import functools
import math

import jax
import jax.numpy as jnp
import ml_dtypes
import numpy as np
from jax import lax
from jax.experimental import pallas as pl
from jax.experimental.pallas import tpu as pltpu
from jax.sharding import PartitionSpec as P

CHEB = 8
RANK = 64
GRID = 4096
LEVELS = 8
START = 2
HALF = 4
LANES = 2 * RANK
F32 = jnp.float32
BF16 = jnp.bfloat16
MIB = 1 << 20

SIN_TERMS = (6.283184916, -41.34158923, 81.59994333, -76.61447253, 41.34288235, -12.47124353)
COS_TERMS = (0.9999999891, -19.7392045, 64.93911746, -85.45013953, 60.16763095, -25.96759925, 6.528658158)


def lagrange_tables(node_count):
    cheb_nodes = 0.5 * np.cos((2.0 * np.arange(node_count) + 1.0) * math.pi / (2.0 * node_count))
    single = np.ones((2, node_count, node_count))
    for child_bit in range(2):
        for source in range(node_count):
            location = (child_bit - 0.5) / 2.0 + cheb_nodes[source] / 2.0
            for target in range(node_count):
                for another in range(node_count):
                    if another != target:
                        single[child_bit, source, target] *= (location - cheb_nodes[another]) / (
                            cheb_nodes[target] - cheb_nodes[another]
                        )
    paired = single[:, None, :, None, :, None] * single[None, :, None, :, None, :]
    paired = paired.reshape(2, 2, node_count * node_count, node_count * node_count)
    return (cheb_nodes, paired)


def mixing_weights():
    table = lagrange_tables(CHEB)[1].astype(np.float32).reshape(4, RANK, RANK)
    high = table.astype(ml_dtypes.bfloat16)
    low = (table - high.astype(np.float32)).astype(ml_dtypes.bfloat16)
    out = np.zeros((4, 2, LANES, 2, LANES), ml_dtypes.bfloat16)
    for half in range(2):
        part = slice(half * RANK, (half + 1) * RANK)
        for split in range(2):
            out[:, split, part, 0, part] = high
            out[:, split, part, 1, part] = low
    return out.reshape(4 * 2 * LANES, 2 * LANES)


def node_lanes():
    nodes = lagrange_tables(CHEB)[0].astype(np.float32)
    lane = np.arange(LANES) % RANK
    out = np.zeros((8, LANES), np.float32)
    out[0] = nodes[lane // CHEB]
    out[1] = nodes[lane % CHEB]
    return out


def poly(terms, u):
    acc = terms[-1] * u + terms[-2]
    for term in terms[-3::-1]:
        acc = acc * u + term
    return acc


def sin_turns(f):
    return f * poly(SIN_TERMS, f * f)


def cos_sin(turns):
    f = turns - jnp.round(turns)
    u = f * f
    return poly(COS_TERMS, u), f * poly(SIN_TERMS, u)


def reversed_bits(values, count):
    out = jnp.zeros_like(values)
    for bit in range(count):
        out = out + (((values >> bit) & 1) << (count - 1 - bit))
    return out


def dim_tables(j, after, index, dim, nodes_ref):
    row = lax.broadcasted_iota(jnp.int32, (16, LANES), 0)
    lane = lax.broadcasted_iota(jnp.int32, (16, LANES), 1)
    half = (lane >= RANK).astype(jnp.int32)
    if dim == 0:
        g = row * 16 + half * 8 + index if after else index * 32 + half * 16 + row
    else:
        g = row * 16 + index if after else index * 16 + row
    z = jnp.broadcast_to(nodes_ref[dim : dim + 1, :], (16, LANES))
    b = g >> j
    p = reversed_bits(g & ((1 << j) - 1), j)
    level = START + j
    width = 2.0**level
    wave = (-GRID / 2.0 + (b.astype(F32) + 0.5) * width) + width * z
    odd = ((2 * b + 1) & 7).astype(F32) * 0.125
    linear = odd + 0.25 * z
    p = p.astype(F32)
    parent = sin_turns((p + 0.5) * 0.5**level)
    new = [sin_turns((2.0 * p + (s + 0.5)) * 0.5 ** (level + 1)) for s in range(2)]
    if j == 0:
        lin = []
        for s in range(2):
            whole = (((2 * b + 1) * (2 * s + 1)) & 7).astype(F32) * 0.125
            lin.append(-(whole + ((2 * s + 1) * 0.25) * z))
    else:
        lin = [linear, -linear]
    return wave, lin, parent, new


def store_tables(ref, dim, tables):
    wave, lin, parent, new = tables
    for k, value in enumerate((wave, lin[0], lin[1], parent, new[0], new[1])):
        ref[dim, k] = value


def fill_phases(j, after, index_one, index_two, nodes_ref, tab_ref, store):
    store_tables(tab_ref, 0, dim_tables(j, after, index_one, 0, nodes_ref))
    store_tables(tab_ref, 1, dim_tables(j, after, index_two, 1, nodes_ref))

    @pl.loop(0, 16)
    def _(i1):
        def one(k):
            return jnp.broadcast_to(tab_ref[0, k, pl.ds(i1, 1), :], (8, LANES))

        wave1 = one(0)
        wave1 = wave1 * wave1
        lin1 = (one(1), one(2))
        par1, new1 = one(3) * 0.0625, (one(4) * 0.0625, one(5) * 0.0625)
        for h in range(2):

            def two(k):
                return tab_ref[1, k, 8 * h : 8 * h + 8, :]

            wave2 = two(0)
            radius = jnp.sqrt(wave1 + wave2 * wave2)
            lin2 = (two(1), two(2))
            par = par1 * two(3)
            for s1 in range(2):
                for s2 in range(2):
                    new = new1[s1] * two(4 + s2)
                    bend = -(0.125 + new) if j == 0 else par - new
                    turns = bend * radius + (lin1[s1] + lin2[s2])
                    cos, sin = cos_sin(turns)
                    store(i1, 2 * s1 + s2, h, cos, sin)


def phase_rows(i1, s, h):
    return pl.ds(pl.multiple_of((i1 * 4 + s) * 16 + 8 * h, 8), 8)


def fill_final(index_one, index_two, nodes_ref, tab_ref, store):
    row = lax.broadcasted_iota(jnp.int32, (16, LANES), 0)
    lane = lax.broadcasted_iota(jnp.int32, (16, LANES), 1)
    half = (lane >= RANK).astype(jnp.int32)
    for dim in range(2):
        g = row * 16 + half * 8 + index_one if dim == 0 else row * 16 + index_two
        z = jnp.broadcast_to(nodes_ref[dim : dim + 1, :], (16, LANES))
        p = 2 * reversed_bits(g, LEVELS) + 1
        level = START + LEVELS
        wave = (-GRID / 2.0 + 0.5 * 2.0**level) + 2.0**level * z
        whole = ((-3 * p) & 3).astype(F32) * 0.25
        tab_ref[dim, 0] = wave
        tab_ref[dim, 1] = whole + (p.astype(F32) * 0.5) * z
        tab_ref[dim, 2] = sin_turns(p.astype(F32) * 0.5 ** (level + 1))

    @pl.loop(0, 16)
    def _(i1):
        def one(k):
            return jnp.broadcast_to(tab_ref[0, k, pl.ds(i1, 1), :], (8, LANES))

        wave1, lin1, sin1 = one(0), one(1), one(2) * 0.0625
        for h in range(2):
            rows = slice(8 * h, 8 * h + 8)
            wave2 = tab_ref[1, 0, rows, :]
            radius = jnp.sqrt(wave1 * wave1 + wave2 * wave2)
            bend = 0.125 + sin1 * tab_ref[1, 2, rows, :]
            turns = bend * radius + (lin1 + tab_ref[1, 1, rows, :])
            turns = turns - jnp.round(turns)
            cos, sin = cos_sin(turns)
            store(i1, h, cos, sin)


def insert(rest, bit, value):
    low = rest & ((1 << bit) - 1)
    return ((rest >> bit) << (bit + 1)) + (value << bit) + low


def turn_signs():
    row = lax.broadcasted_iota(jnp.int32, (8, LANES), 0)
    return jnp.where(row < 4, -1.0, 1.0).astype(F32)


def level(bit, place, load, cos_of, sin_of, lhs_ref, w_ref, emit):
    signs = turn_signs()

    @pl.loop(0, 8)
    def _(r1):
        for r2 in range(8):
            for c in range(4):
                i1 = insert(r1, bit, c >> 1)
                i2 = insert(r2, bit, c & 1)
                value = load(place(i1, i2))
                turned = pltpu.roll(value, 4, 0) * signs
                for s1 in range(2):
                    parts = []
                    for s2 in range(2):
                        row = (i1 * 4 + (2 * s1 + s2)) * 16 + i2
                        cos = cos_of(row)
                        sin = sin_of(row)
                        parts.append(value * cos + turned * sin)
                    both = jnp.concatenate(parts, axis=0)
                    high = both.astype(BF16)
                    low = (both - high.astype(F32)).astype(BF16)
                    start = pl.multiple_of(r1 * 256 + (r2 * 2 + s1) * 16, 16)
                    lhs_ref[pl.ds(start, 16), 256 * c : 256 * c + 128] = high
                    lhs_ref[pl.ds(start, 16), 256 * c + 128 : 256 * c + 256] = low

    @pl.loop(0, 4)
    def _(block):
        y = jnp.dot(
            lhs_ref[pl.ds(pl.multiple_of(block * 512, 512), 512), :],
            w_ref[...],
            preferred_element_type=F32,
        )
        y = y[:, :LANES] + y[:, LANES:]
        for q in range(2):
            r1 = block * 2 + q
            for r2 in range(8):
                base = (q * 8 + r2) * 32
                new = [y[base + 8 * s : base + 8 * s + 8] for s in range(4)]
                emit(r1, r2, new)


def before_kernel(x_ref, w_ref, nodes_ref, out_ref, d0, d1, cos_ref, sin_ref, tab_ref, lhs_ref):
    index_one = lax.axis_index("sx")
    index_two = lax.axis_index("sy")
    lower = lax.broadcasted_iota(jnp.int32, (8, LANES), 1) < RANK

    @pl.loop(0, 16)
    def _(i1):
        for part in range(2):
            for h in range(2):
                for pair in range(2):
                    cols = slice(pair * LANES, (pair + 1) * LANES)
                    a = x_ref[part, pl.ds(i1, 1), 8 * h : 8 * h + 8, cols].reshape(8, LANES)
                    b = x_ref[part, pl.ds(i1 + 16, 1), 8 * h : 8 * h + 8, cols].reshape(8, LANES)
                    start = (i1 * 16 + 8 * h) * 8 + part * 4 + 2 * pair
                    d0[pl.ds(start, 8, stride=8), :] = jnp.where(lower, a, pltpu.roll(b, RANK, 1))
                    d0[pl.ds(start + 1, 8, stride=8), :] = jnp.where(lower, pltpu.roll(a, RANK, 1), b)

    def place(i1, i2):
        return i1 * 16 + i2

    refs = (d0, d1)
    for j in range(HALF):

        def store(i1, s, h, cos, sin):
            cos_ref[phase_rows(i1, s, h), :] = cos
            sin_ref[phase_rows(i1, s, h), :] = sin

        fill_phases(j, False, index_one, index_two, nodes_ref, tab_ref, store)
        source, target = refs[j % 2], refs[(j + 1) % 2]

        def load(pos):
            return source[pl.ds(pl.multiple_of(pos * 8, 8), 8), :]

        def emit(r1, r2, new):
            if j < HALF - 1:
                for s in range(4):
                    pos = place(insert(r1, j, s >> 1), insert(r2, j, s & 1))
                    target[pl.ds(pl.multiple_of(pos * 8, 8), 8), :] = new[s]
            else:
                for s2 in range(2):
                    a, b = new[s2], new[2 + s2]
                    pos = ((r1 * 16 + insert(r2, j, s2)) * 2) * 8
                    first = jnp.where(lower, a, pltpu.roll(b, RANK, 1))
                    second = jnp.where(lower, pltpu.roll(a, RANK, 1), b)
                    out_ref[pl.ds(pl.multiple_of(pos, 8), 8), :] = first
                    out_ref[pl.ds(pl.multiple_of(pos + 8, 8), 8), :] = second

        level(
            j,
            place,
            load,
            lambda row: cos_ref[pl.ds(row, 1), :],
            lambda row: sin_ref[pl.ds(row, 1), :],
            lhs_ref,
            w_ref,
            emit,
        )


def phases_kernel(nodes_ref, cos_ref, sin_ref, cosf_ref, sinf_ref, tab_ref):
    index_one = lax.axis_index("sx")
    index_two = lax.axis_index("sy")
    for step in range(LEVELS - HALF):

        def store(i1, s, h, cos, sin):
            cos_ref[step, phase_rows(i1, s, h), :] = cos
            sin_ref[step, phase_rows(i1, s, h), :] = sin

        fill_phases(HALF + step, True, index_one, index_two, nodes_ref, tab_ref, store)

    def store_final(i1, h, cos, sin):
        rows = pl.ds(pl.multiple_of(i1 * 16 + 8 * h, 8), 8)
        cosf_ref[rows, :] = cos
        sinf_ref[rows, :] = sin

    fill_final(index_one, index_two, nodes_ref, tab_ref, store_final)


def after_kernel(x_ref, w_ref, cos_ref, sin_ref, cosf_ref, sinf_ref, out_ref, d0, d1, lhs_ref):
    def place(i1, i2):
        return (i1 >> 1) * 32 + i2 * 2 + (i1 & 1)

    signs = turn_signs()
    refs = (x_ref, d0, d1, d0, out_ref)
    for step in range(LEVELS - HALF):
        source, target = refs[step], refs[step + 1]

        def load(pos):
            return source[pl.ds(pl.multiple_of(pos * 8, 8), 8), :]

        def emit(r1, r2, new):
            for s in range(4):
                i1, i2 = insert(r1, step, s >> 1), insert(r2, step, s & 1)
                value = new[s]
                if step == LEVELS - HALF - 1:
                    row = i1 * 16 + i2
                    cos, sin = cosf_ref[pl.ds(row, 1), :], sinf_ref[pl.ds(row, 1), :]
                    value = value * cos + (pltpu.roll(value, 4, 0) * signs) * sin
                target[pl.ds(pl.multiple_of(place(i1, i2) * 8, 8), 8), :] = value

        level(
            step,
            place,
            load,
            lambda row: cos_ref[step, pl.ds(row, 1), :],
            lambda row: sin_ref[step, pl.ds(row, 1), :],
            lhs_ref,
            w_ref,
            emit,
        )


def order_kernel(x_ref, out_ref):
    lower = lax.broadcasted_iota(jnp.int32, (8, LANES), 1) < RANK

    @pl.loop(0, 8)
    def _(sx):
        for b4 in range(2):
            for part in range(2):
                for pair in range(2):
                    cols = slice(pair * LANES, (pair + 1) * LANES)
                    for h in range(2):
                        start = ((sx * 16 + 8 * h) * 2 + b4) * 8 + part * 4 + 2 * pair
                        a = x_ref[pl.ds(start, 8, stride=16), :]
                        b = x_ref[pl.ds(start + 1, 8, stride=16), :]
                        first = jnp.where(lower, a, pltpu.roll(b, RANK, 1))
                        second = jnp.where(lower, pltpu.roll(a, RANK, 1), b)
                        rows = slice(8 * h, 8 * h + 8)
                        out_ref[part, pl.ds(b4 * 16 + sx, 1), rows, cols] = first[None]
                        out_ref[part, pl.ds(b4 * 16 + 8 + sx, 1), rows, cols] = second[None]


VMEM = pl.BlockSpec(memory_space=pltpu.VMEM)
ROWS = 2048


def local(weights):
    w = jnp.asarray(mixing_weights())
    nodes = jnp.asarray(node_lanes())
    shape = jax.ShapeDtypeStruct((ROWS, LANES), F32)
    values = pltpu.VMEM((ROWS, LANES), F32)
    table = pltpu.VMEM((2, 6, 16, LANES), F32)
    lhs = pltpu.VMEM((2048, 1024), BF16)
    cost = functools.partial(pl.CostEstimate, transcendentals=0)

    before = pl.pallas_call(
        before_kernel,
        out_shape=shape,
        in_specs=[VMEM] * 3,
        out_specs=VMEM,
        scratch_shapes=[values, values, pltpu.VMEM((1024, LANES), F32), pltpu.VMEM((1024, LANES), F32), table, lhs],
        compiler_params=pltpu.CompilerParams(vmem_limit_bytes=24 * MIB),
        cost_estimate=cost(flops=4 * 2**31, bytes_accessed=3 * MIB),
        name="before",
    )(weights, w, nodes)

    moved = lax.all_to_all(before.reshape(128, 16, LANES), ("sx", "sy"), 0, 0, tiled=True)

    phase = jax.ShapeDtypeStruct((LEVELS - HALF, 1024, LANES), F32)
    last = jax.ShapeDtypeStruct((256, LANES), F32)
    phases = pl.pallas_call(
        phases_kernel,
        out_shape=(phase, phase, last, last),
        in_specs=[VMEM],
        out_specs=(VMEM,) * 4,
        scratch_shapes=[table],
        compiler_params=pltpu.CompilerParams(vmem_limit_bytes=24 * MIB),
        cost_estimate=cost(flops=2**33, bytes_accessed=5 * MIB),
        name="phases",
    )(nodes)

    after = pl.pallas_call(
        after_kernel,
        out_shape=shape,
        in_specs=[VMEM] * 6,
        out_specs=VMEM,
        scratch_shapes=[values, values, lhs],
        compiler_params=pltpu.CompilerParams(vmem_limit_bytes=24 * MIB),
        cost_estimate=cost(flops=4 * 2**31, bytes_accessed=8 * MIB),
        name="after",
    )(moved.reshape(ROWS, LANES), w, *phases)

    moved = lax.all_to_all(after.reshape(128, 16, LANES), ("sx", "sy"), 0, 0, tiled=True)

    return pl.pallas_call(
        order_kernel,
        out_shape=jax.ShapeDtypeStruct(weights.shape, F32),
        in_specs=[VMEM],
        out_specs=VMEM,
        compiler_params=pltpu.CompilerParams(vmem_limit_bytes=8 * MIB),
        cost_estimate=cost(flops=2**20, bytes_accessed=2 * MIB),
        name="order",
    )(moved.reshape(ROWS, LANES))


def solution(mesh):
    return jax.shard_map(
        local,
        mesh=mesh,
        in_specs=(P(None, "sx", "sy", None),),
        out_specs=P(None, "sx", "sy", None),
        check_vma=False,
    )
```

```python
import functools
import math

import jax
import jax.numpy as jnp
import ml_dtypes
import numpy as np
from jax import lax
from jax.experimental import pallas as pl
from jax.experimental.pallas import tpu as pltpu
from jax.sharding import PartitionSpec as P

CHEB = 8
RANK = 64
GRID = 4096
LEVELS = 8
START = 2
HALF = 4
LANES = 2 * RANK
F32 = jnp.float32
BF16 = jnp.bfloat16
MIB = 1 << 20
SPAN = 2

SIN_TERMS = (6.283184916, -41.34158923, 81.59994333, -76.61447253, 41.34288235, -12.47124353)
COS_TERMS = (0.9999999891, -19.7392045, 64.93911746, -85.45013953, 60.16763095, -25.96759925, 6.528658158)


def lagrange_tables(node_count):
    cheb_nodes = 0.5 * np.cos((2.0 * np.arange(node_count) + 1.0) * math.pi / (2.0 * node_count))
    single = np.ones((2, node_count, node_count))
    for child_bit in range(2):
        for source in range(node_count):
            location = (child_bit - 0.5) / 2.0 + cheb_nodes[source] / 2.0
            for target in range(node_count):
                for another in range(node_count):
                    if another != target:
                        single[child_bit, source, target] *= (location - cheb_nodes[another]) / (
                            cheb_nodes[target] - cheb_nodes[another]
                        )
    paired = single[:, None, :, None, :, None] * single[None, :, None, :, None, :]
    paired = paired.reshape(2, 2, node_count * node_count, node_count * node_count)
    return (cheb_nodes, paired)


def mixing_weights():
    table = lagrange_tables(CHEB)[1].astype(np.float32).reshape(4, RANK, RANK)
    high = table.astype(ml_dtypes.bfloat16)
    low = (table - high.astype(np.float32)).astype(ml_dtypes.bfloat16)
    out = np.zeros((4, 2, LANES, 2, LANES), ml_dtypes.bfloat16)
    for half in range(2):
        part = slice(half * RANK, (half + 1) * RANK)
        for split in range(2):
            out[:, split, part, 0, part] = high
            out[:, split, part, 1, part] = low
    return out.reshape(4 * 2 * LANES, 2 * LANES)


def node_values(lane, dim):
    nodes = lagrange_tables(CHEB)[0].astype(np.float32)
    point = lane & (RANK - 1)
    which = point >> 3 if dim == 0 else point & 7
    out = jnp.full(lane.shape, float(nodes[0]), F32)
    for k in range(1, CHEB):
        out = jnp.where(which == k, float(nodes[k]), out)
    return out


def poly(terms, u):
    acc = terms[-1] * u + terms[-2]
    for term in terms[-3::-1]:
        acc = acc * u + term
    return acc


def sin_turns(f):
    return f * poly(SIN_TERMS, f * f)


def cos_sin(turns):
    f = turns - jnp.round(turns)
    u = f * f
    return poly(COS_TERMS, u), f * poly(SIN_TERMS, u)


def reversed_bits(values, count):
    out = jnp.zeros_like(values)
    for bit in range(count):
        out = out + (((values >> bit) & 1) << (count - 1 - bit))
    return out


def dim_tables(j, after, index, dim):
    row = lax.broadcasted_iota(jnp.int32, (16, LANES), 0)
    lane = lax.broadcasted_iota(jnp.int32, (16, LANES), 1)
    half = (lane >= RANK).astype(jnp.int32)
    if dim == 0:
        g = row * 16 + half * 8 + index if after else index * 32 + half * 16 + row
    else:
        g = row * 16 + index if after else index * 16 + row
    z = node_values(lane, dim)
    b = g >> j
    p = reversed_bits(g & ((1 << j) - 1), j)
    level = START + j
    width = 2.0**level
    wave = (-GRID / 2.0 + (b.astype(F32) + 0.5) * width) + width * z
    odd = ((2 * b + 1) & 7).astype(F32) * 0.125
    linear = odd + 0.25 * z
    p = p.astype(F32)
    parent = sin_turns((p + 0.5) * 0.5**level)
    new = [sin_turns((2.0 * p + (s + 0.5)) * 0.5 ** (level + 1)) for s in range(2)]
    if j == 0:
        lin = []
        for s in range(2):
            whole = (((2 * b + 1) * (2 * s + 1)) & 7).astype(F32) * 0.125
            lin.append(-(whole + ((2 * s + 1) * 0.25) * z))
    else:
        lin = [linear, -linear]
    return wave, lin, parent, new


def store_tables(ref, dim, tables):
    wave, lin, parent, new = tables
    for k, value in enumerate((wave, lin[0], lin[1], parent, new[0], new[1])):
        ref[dim, k] = value


def fill_phases(j, after, index_one, index_two, tab_ref, store):
    store_tables(tab_ref, 0, dim_tables(j, after, index_one, 0))
    store_tables(tab_ref, 1, dim_tables(j, after, index_two, 1))

    @pl.loop(0, 16)
    def _(i1):
        def one(k):
            return jnp.broadcast_to(tab_ref[0, k, pl.ds(i1, 1), :], (8, LANES))

        wave1 = one(0)
        wave1 = wave1 * wave1
        lin1 = (one(1), one(2))
        par1, new1 = one(3) * 0.0625, (one(4) * 0.0625, one(5) * 0.0625)
        for h in range(2):

            def two(k):
                return tab_ref[1, k, 8 * h : 8 * h + 8, :]

            wave2 = two(0)
            radius = jnp.sqrt(wave1 + wave2 * wave2)
            lin2 = (two(1), two(2))
            par = par1 * two(3)
            for s1 in range(2):
                for s2 in range(2):
                    new = new1[s1] * two(4 + s2)
                    bend = -(0.125 + new) if j == 0 else par - new
                    turns = bend * radius + (lin1[s1] + lin2[s2])
                    cos, sin = cos_sin(turns)
                    store(i1, 2 * s1 + s2, h, cos, sin)


def phase_rows(i1, s, h):
    return pl.ds(pl.multiple_of((i1 * 4 + s) * 16 + 8 * h, 8), 8)


def fill_final(index_one, index_two, tab_ref, store):
    row = lax.broadcasted_iota(jnp.int32, (16, LANES), 0)
    lane = lax.broadcasted_iota(jnp.int32, (16, LANES), 1)
    half = (lane >= RANK).astype(jnp.int32)
    for dim in range(2):
        g = row * 16 + half * 8 + index_one if dim == 0 else row * 16 + index_two
        z = node_values(lane, dim)
        p = 2 * reversed_bits(g, LEVELS) + 1
        level = START + LEVELS
        wave = (-GRID / 2.0 + 0.5 * 2.0**level) + 2.0**level * z
        whole = ((-3 * p) & 3).astype(F32) * 0.25
        tab_ref[dim, 0] = wave
        tab_ref[dim, 1] = whole + (p.astype(F32) * 0.5) * z
        tab_ref[dim, 2] = sin_turns(p.astype(F32) * 0.5 ** (level + 1))

    @pl.loop(0, 16)
    def _(i1):
        def one(k):
            return jnp.broadcast_to(tab_ref[0, k, pl.ds(i1, 1), :], (8, LANES))

        wave1, lin1, sin1 = one(0), one(1), one(2) * 0.0625
        for h in range(2):
            rows = slice(8 * h, 8 * h + 8)
            wave2 = tab_ref[1, 0, rows, :]
            radius = jnp.sqrt(wave1 * wave1 + wave2 * wave2)
            bend = 0.125 + sin1 * tab_ref[1, 2, rows, :]
            turns = bend * radius + (lin1 + tab_ref[1, 1, rows, :])
            turns = turns - jnp.round(turns)
            cos, sin = cos_sin(turns)
            store(i1, h, cos, sin)


def insert(rest, bit, value):
    low = rest & ((1 << bit) - 1)
    return ((rest >> bit) << (bit + 1)) + (value << bit) + low


def turn_signs():
    row = lax.broadcasted_iota(jnp.int32, (8, LANES), 0)
    return jnp.where(row < 4, -1.0, 1.0).astype(F32)


def level(bit, place, load, cos_of, sin_of, lhs_refs, w_ref, emit, beside=None):
    signs = turn_signs()

    def build(chunk, lhs_ref):
        for q in range(SPAN):
            r1 = chunk * SPAN + q
            for r2 in range(8):
                for c in range(4):
                    i1 = insert(r1, bit, c >> 1)
                    i2 = insert(r2, bit, c & 1)
                    value = load(place(i1, i2))
                    turned = pltpu.roll(value, 4, 0) * signs
                    for s1 in range(2):
                        parts = []
                        for s2 in range(2):
                            row = (i1 * 4 + (2 * s1 + s2)) * 16 + i2
                            parts.append(value * cos_of(row) + turned * sin_of(row))
                        both = jnp.concatenate(parts, axis=0)
                        high = both.astype(BF16)
                        low = (both - high.astype(F32)).astype(BF16)
                        start = q * 256 + (r2 * 2 + s1) * 16
                        lhs_ref[start : start + 16, 256 * c : 256 * c + 128] = high
                        lhs_ref[start : start + 16, 256 * c + 128 : 256 * c + 256] = low

    def multiply(chunk, lhs_ref):
        y = jnp.dot(lhs_ref[...], w_ref[...], preferred_element_type=F32)
        y = y[:, :LANES] + y[:, LANES:]
        for q in range(SPAN):
            for r2 in range(8):
                base = (q * 8 + r2) * 32
                new = [y[base + 8 * s : base + 8 * s + 8] for s in range(4)]
                emit(chunk * SPAN + q, r2, new)

    chunks = 8 // SPAN
    first, second = lhs_refs
    build(0, first)

    @pl.loop(0, chunks // 2 - 1)
    def _(k):
        multiply(2 * k, first)
        build(2 * k + 1, second)
        multiply(2 * k + 1, second)
        build(2 * k + 2, first)

    multiply(chunks - 2, first)
    build(chunks - 1, second)
    multiply(chunks - 1, second)


def before_kernel(x_hbm, w_hbm, out_ref, x_ref, w_ref, d0, d1, cos_ref, sin_ref, tab_ref, lhs0, lhs1, sems):
    copy_x = pltpu.make_async_copy(x_hbm, x_ref, sems.at[0])
    copy_w = pltpu.make_async_copy(w_hbm, w_ref, sems.at[1])
    copy_x.start()
    copy_w.start()
    index_one = lax.axis_index("sx")
    index_two = lax.axis_index("sy")
    lower = lax.broadcasted_iota(jnp.int32, (8, LANES), 1) < RANK

    def place(i1, i2):
        return i1 * 16 + i2

    refs = (d0, d1)
    for j in range(HALF):

        def store(i1, s, h, cos, sin):
            cos_ref[phase_rows(i1, s, h), :] = cos
            sin_ref[phase_rows(i1, s, h), :] = sin

        fill_phases(j, False, index_one, index_two, tab_ref, store)
        if j == 0:
            copy_x.wait()

            @pl.loop(0, 16)
            def _(i1):
                for part in range(2):
                    for h in range(2):
                        for pair in range(2):
                            cols = slice(pair * LANES, (pair + 1) * LANES)
                            a = x_ref[part, pl.ds(i1, 1), 8 * h : 8 * h + 8, cols].reshape(8, LANES)
                            b = x_ref[part, pl.ds(i1 + 16, 1), 8 * h : 8 * h + 8, cols].reshape(8, LANES)
                            start = (i1 * 16 + 8 * h) * 8 + part * 4 + 2 * pair
                            d0[pl.ds(start, 8, stride=8), :] = jnp.where(lower, a, pltpu.roll(b, RANK, 1))
                            d0[pl.ds(start + 1, 8, stride=8), :] = jnp.where(lower, pltpu.roll(a, RANK, 1), b)

            copy_w.wait()
        source, target = refs[j % 2], refs[(j + 1) % 2]

        def load(pos):
            return source[pl.ds(pl.multiple_of(pos * 8, 8), 8), :]

        def emit(r1, r2, new):
            if j < HALF - 1:
                for s in range(4):
                    pos = place(insert(r1, j, s >> 1), insert(r2, j, s & 1))
                    target[pl.ds(pl.multiple_of(pos * 8, 8), 8), :] = new[s]
            else:
                for s2 in range(2):
                    a, b = new[s2], new[2 + s2]
                    pos = ((r1 * 16 + insert(r2, j, s2)) * 2) * 8
                    first = jnp.where(lower, a, pltpu.roll(b, RANK, 1))
                    second = jnp.where(lower, pltpu.roll(a, RANK, 1), b)
                    out_ref[pl.ds(pl.multiple_of(pos, 8), 8), :] = first
                    out_ref[pl.ds(pl.multiple_of(pos + 8, 8), 8), :] = second

        level(
            j,
            place,
            load,
            lambda row: cos_ref[pl.ds(row, 1), :],
            lambda row: sin_ref[pl.ds(row, 1), :],
            (lhs0, lhs1),
            w_ref,
            emit,
        )


def phases_kernel(cos_ref, sin_ref, cosf_ref, sinf_ref, tab_ref):
    index_one = lax.axis_index("sx")
    index_two = lax.axis_index("sy")
    for step in range(LEVELS - HALF):

        def store(i1, s, h, cos, sin):
            cos_ref[step, phase_rows(i1, s, h), :] = cos
            sin_ref[step, phase_rows(i1, s, h), :] = sin

        fill_phases(HALF + step, True, index_one, index_two, tab_ref, store)

    def store_final(i1, h, cos, sin):
        rows = pl.ds(pl.multiple_of(i1 * 16 + 8 * h, 8), 8)
        cosf_ref[rows, :] = cos
        sinf_ref[rows, :] = sin

    fill_final(index_one, index_two, tab_ref, store_final)


def after_kernel(x_hbm, w_hbm, cos_hbm, sin_hbm, cosf_hbm, sinf_hbm, out_ref, *scratch):
    x_ref, w_ref, cos_ref, sin_ref, cosf_ref, sinf_ref, d0, d1, lhs0, lhs1, sems = scratch
    steps = LEVELS - HALF
    copy_w = pltpu.make_async_copy(w_hbm, w_ref, sems.at[2 * steps])
    copies = [
        (
            pltpu.make_async_copy(cos_hbm.at[k], cos_ref.at[k], sems.at[2 * k]),
            pltpu.make_async_copy(sin_hbm.at[k], sin_ref.at[k], sems.at[2 * k + 1]),
        )
        for k in range(steps)
    ]
    copies[-1] += (
        pltpu.make_async_copy(cosf_hbm, cosf_ref, sems.at[2 * steps + 1]),
        pltpu.make_async_copy(sinf_hbm, sinf_ref, sems.at[2 * steps + 2]),
    )
    copies[0] += (copy_w, pltpu.make_async_copy(x_hbm, x_ref, sems.at[2 * steps + 3]))
    for group in copies:
        for copy in group:
            copy.start()

    def place(i1, i2):
        return (i1 >> 1) * 32 + i2 * 2 + (i1 & 1)

    signs = turn_signs()
    refs = (x_ref, d0, d1, d0, out_ref)
    for step in range(LEVELS - HALF):
        for copy in copies[step]:
            copy.wait()
        source, target = refs[step], refs[step + 1]

        def load(pos):
            return source[pl.ds(pl.multiple_of(pos * 8, 8), 8), :]

        def emit(r1, r2, new):
            for s in range(4):
                i1, i2 = insert(r1, step, s >> 1), insert(r2, step, s & 1)
                value = new[s]
                if step == LEVELS - HALF - 1:
                    row = i1 * 16 + i2
                    cos, sin = cosf_ref[pl.ds(row, 1), :], sinf_ref[pl.ds(row, 1), :]
                    value = value * cos + (pltpu.roll(value, 4, 0) * signs) * sin
                target[pl.ds(pl.multiple_of(place(i1, i2) * 8, 8), 8), :] = value

        level(
            step,
            place,
            load,
            lambda row: cos_ref[step, pl.ds(row, 1), :],
            lambda row: sin_ref[step, pl.ds(row, 1), :],
            (lhs0, lhs1),
            w_ref,
            emit,
        )


def order_kernel(x_ref, out_ref):
    lower = lax.broadcasted_iota(jnp.int32, (8, LANES), 1) < RANK

    @pl.loop(0, 8)
    def _(sx):
        for b4 in range(2):
            for part in range(2):
                for pair in range(2):
                    cols = slice(pair * LANES, (pair + 1) * LANES)
                    for h in range(2):
                        start = ((sx * 16 + 8 * h) * 2 + b4) * 8 + part * 4 + 2 * pair
                        a = x_ref[pl.ds(start, 8, stride=16), :]
                        b = x_ref[pl.ds(start + 1, 8, stride=16), :]
                        first = jnp.where(lower, a, pltpu.roll(b, RANK, 1))
                        second = jnp.where(lower, pltpu.roll(a, RANK, 1), b)
                        rows = slice(8 * h, 8 * h + 8)
                        out_ref[part, pl.ds(b4 * 16 + sx, 1), rows, cols] = first[None]
                        out_ref[part, pl.ds(b4 * 16 + 8 + sx, 1), rows, cols] = second[None]


VMEM = pl.BlockSpec(memory_space=pltpu.VMEM)
ANY = pl.BlockSpec(memory_space=pl.ANY)
ROWS = 2048


def local(weights):
    w = jnp.asarray(mixing_weights())
    shape = jax.ShapeDtypeStruct((ROWS, LANES), F32)
    values = pltpu.VMEM((ROWS, LANES), F32)
    table = pltpu.VMEM((2, 6, 16, LANES), F32)
    lhs = pltpu.VMEM((256 * SPAN, 1024), BF16)
    mixing = pltpu.VMEM((1024, 2 * LANES), BF16)
    cost = functools.partial(pl.CostEstimate, transcendentals=0)

    before = pl.pallas_call(
        before_kernel,
        out_shape=shape,
        in_specs=[ANY, ANY],
        out_specs=VMEM,
        scratch_shapes=[
            pltpu.VMEM(weights.shape, F32),
            mixing,
            values,
            values,
            pltpu.VMEM((1024, LANES), F32),
            pltpu.VMEM((1024, LANES), F32),
            table,
            lhs,
            lhs,
            pltpu.SemaphoreType.DMA((2,)),
        ],
        compiler_params=pltpu.CompilerParams(vmem_limit_bytes=59 * MIB),
        cost_estimate=cost(flops=4 * 2**31, bytes_accessed=3 * MIB),
        name="before",
    )(weights, w)

    moved = lax.all_to_all(before.reshape(128, 16, LANES), ("sx", "sy"), 0, 0, tiled=True)

    phase = jax.ShapeDtypeStruct((LEVELS - HALF, 1024, LANES), F32)
    last = jax.ShapeDtypeStruct((256, LANES), F32)
    phases = pl.pallas_call(
        phases_kernel,
        out_shape=(phase, phase, last, last),
        in_specs=[],
        out_specs=(VMEM,) * 4,
        scratch_shapes=[table],
        compiler_params=pltpu.CompilerParams(vmem_limit_bytes=24 * MIB),
        cost_estimate=cost(flops=2**33, bytes_accessed=5 * MIB),
        name="phases",
    )()

    after = pl.pallas_call(
        after_kernel,
        out_shape=shape,
        in_specs=[ANY] * 6,
        out_specs=VMEM,
        scratch_shapes=[
            values,
            mixing,
            pltpu.VMEM(phase.shape, F32),
            pltpu.VMEM(phase.shape, F32),
            pltpu.VMEM(last.shape, F32),
            pltpu.VMEM(last.shape, F32),
            values,
            values,
            lhs,
            lhs,
            pltpu.SemaphoreType.DMA((2 * (LEVELS - HALF) + 4,)),
        ],
        compiler_params=pltpu.CompilerParams(vmem_limit_bytes=59 * MIB),
        cost_estimate=cost(flops=4 * 2**31, bytes_accessed=8 * MIB),
        name="after",
    )(moved.reshape(ROWS, LANES), w, *phases)

    moved = lax.all_to_all(after.reshape(128, 16, LANES), ("sx", "sy"), 0, 0, tiled=True)

    return pl.pallas_call(
        order_kernel,
        out_shape=jax.ShapeDtypeStruct(weights.shape, F32),
        in_specs=[VMEM],
        out_specs=VMEM,
        compiler_params=pltpu.CompilerParams(vmem_limit_bytes=8 * MIB),
        cost_estimate=cost(flops=2**20, bytes_accessed=2 * MIB),
        name="order",
    )(moved.reshape(ROWS, LANES))


def solution(mesh):
    return jax.shard_map(
        local,
        mesh=mesh,
        in_specs=(P(None, "sx", "sy", None),),
        out_specs=P(None, "sx", "sy", None),
        check_vma=False,
    )
```

```python
import functools
import math

import jax
import jax.numpy as jnp
import ml_dtypes
import numpy as np
from jax import lax
from jax.experimental import pallas as pl
from jax.experimental.pallas import tpu as pltpu
from jax.sharding import PartitionSpec as P

CHEB = 8
RANK = 64
GRID = 4096
LEVELS = 8
START = 2
HALF = 4
LANES = 2 * RANK
F32 = jnp.float32
BF16 = jnp.bfloat16
MIB = 1 << 20
STEP_ROWS = 1024
PHASE_ROWS = (LEVELS - HALF) * STEP_ROWS + 256

SIN_TERMS = (6.283184916, -41.34158923, 81.59994333, -76.61447253, 41.34288235, -12.47124353)
COS_TERMS = (0.9999999891, -19.7392045, 64.93911746, -85.45013953, 60.16763095, -25.96759925, 6.528658158)


def lagrange_tables(node_count):
    cheb_nodes = 0.5 * np.cos((2.0 * np.arange(node_count) + 1.0) * math.pi / (2.0 * node_count))
    single = np.ones((2, node_count, node_count))
    for child_bit in range(2):
        for source in range(node_count):
            location = (child_bit - 0.5) / 2.0 + cheb_nodes[source] / 2.0
            for target in range(node_count):
                for another in range(node_count):
                    if another != target:
                        single[child_bit, source, target] *= (location - cheb_nodes[another]) / (
                            cheb_nodes[target] - cheb_nodes[another]
                        )
    paired = single[:, None, :, None, :, None] * single[None, :, None, :, None, :]
    paired = paired.reshape(2, 2, node_count * node_count, node_count * node_count)
    return (cheb_nodes, paired)


def mixing_weights():
    table = lagrange_tables(CHEB)[1].astype(np.float32).reshape(4, RANK, RANK)
    high = table.astype(ml_dtypes.bfloat16)
    low = (table - high.astype(np.float32)).astype(ml_dtypes.bfloat16)
    out = np.zeros((4, 2, LANES, 2, LANES), ml_dtypes.bfloat16)
    for half in range(2):
        part = slice(half * RANK, (half + 1) * RANK)
        for split in range(2):
            out[:, split, part, 0, part] = high
            out[:, split, part, 1, part] = low
    return out.reshape(4 * 2 * LANES, 2 * LANES)


def node_values(lane, dim):
    nodes = lagrange_tables(CHEB)[0].astype(np.float32)
    point = lane & (RANK - 1)
    which = point >> 3 if dim == 0 else point & 7
    out = jnp.full(lane.shape, float(nodes[0]), F32)
    for k in range(1, CHEB):
        out = jnp.where(which == k, float(nodes[k]), out)
    return out


def poly(terms, u):
    acc = terms[-1] * u + terms[-2]
    for term in terms[-3::-1]:
        acc = acc * u + term
    return acc


def sin_turns(f):
    return f * poly(SIN_TERMS, f * f)


def cos_sin(turns):
    f = turns - jnp.round(turns)
    u = f * f
    return poly(COS_TERMS, u), f * poly(SIN_TERMS, u)


def reversed_bits(values, count):
    out = jnp.zeros_like(values)
    for bit in range(count):
        out = out + (((values >> bit) & 1) << (count - 1 - bit))
    return out


def dim_tables(j, after, index, dim):
    row = lax.broadcasted_iota(jnp.int32, (16, LANES), 0)
    lane = lax.broadcasted_iota(jnp.int32, (16, LANES), 1)
    half = (lane >= RANK).astype(jnp.int32)
    if dim == 0:
        g = row * 16 + half * 8 + index if after else index * 32 + half * 16 + row
    else:
        g = row * 16 + index if after else index * 16 + row
    z = node_values(lane, dim)
    b = g >> j
    p = reversed_bits(g & ((1 << j) - 1), j)
    level = START + j
    width = 2.0**level
    wave = (-GRID / 2.0 + (b.astype(F32) + 0.5) * width) + width * z
    odd = ((2 * b + 1) & 7).astype(F32) * 0.125
    linear = odd + 0.25 * z
    p = p.astype(F32)
    parent = sin_turns((p + 0.5) * 0.5**level)
    new = [sin_turns((2.0 * p + (s + 0.5)) * 0.5 ** (level + 1)) for s in range(2)]
    if j == 0:
        lin = []
        for s in range(2):
            whole = (((2 * b + 1) * (2 * s + 1)) & 7).astype(F32) * 0.125
            lin.append(-(whole + ((2 * s + 1) * 0.25) * z))
    else:
        lin = [linear, -linear]
    return wave, lin, parent, new


def store_tables(ref, dim, tables):
    wave, lin, parent, new = tables
    for k, value in enumerate((wave, lin[0], lin[1], parent, new[0], new[1])):
        ref[dim, k] = value


def fill_tables(j, after, index_one, index_two, tab_ref):
    store_tables(tab_ref, 0, dim_tables(j, after, index_one, 0))
    store_tables(tab_ref, 1, dim_tables(j, after, index_two, 1))


def phases_at(i1, j, tab_ref, store):
    def one(k):
        return jnp.broadcast_to(tab_ref[0, k, pl.ds(i1, 1), :], (8, LANES))

    wave1 = one(0)
    wave1 = wave1 * wave1
    lin1 = (one(1), one(2))
    par1, new1 = one(3) * 0.0625, (one(4) * 0.0625, one(5) * 0.0625)
    for h in range(2):

        def two(k):
            return tab_ref[1, k, 8 * h : 8 * h + 8, :]

        wave2 = two(0)
        radius = jnp.sqrt(wave1 + wave2 * wave2)
        lin2 = (two(1), two(2))
        par = par1 * two(3)
        for s1 in range(2):
            for s2 in range(2):
                new = new1[s1] * two(4 + s2)
                bend = -(0.125 + new) if j == 0 else par - new
                turns = bend * radius + (lin1[s1] + lin2[s2])
                cos, sin = cos_sin(turns)
                store(i1, 2 * s1 + s2, h, cos, sin)


def fill_phases(j, after, index_one, index_two, tab_ref, store):
    fill_tables(j, after, index_one, index_two, tab_ref)

    @pl.loop(0, 16)
    def _(i1):
        phases_at(i1, j, tab_ref, store)


def phase_rows(i1, s, h):
    start = (i1 * 4 + s) * 16 + 8 * h
    return pl.ds(start if isinstance(start, int) else pl.multiple_of(start, 8), 8)


def fill_final(index_one, index_two, tab_ref, store):
    row = lax.broadcasted_iota(jnp.int32, (16, LANES), 0)
    lane = lax.broadcasted_iota(jnp.int32, (16, LANES), 1)
    half = (lane >= RANK).astype(jnp.int32)
    for dim in range(2):
        g = row * 16 + half * 8 + index_one if dim == 0 else row * 16 + index_two
        z = node_values(lane, dim)
        p = 2 * reversed_bits(g, LEVELS) + 1
        level = START + LEVELS
        wave = (-GRID / 2.0 + 0.5 * 2.0**level) + 2.0**level * z
        whole = ((-3 * p) & 3).astype(F32) * 0.25
        tab_ref[dim, 0] = wave
        tab_ref[dim, 1] = whole + (p.astype(F32) * 0.5) * z
        tab_ref[dim, 2] = sin_turns(p.astype(F32) * 0.5 ** (level + 1))

    @pl.loop(0, 16)
    def _(i1):
        def one(k):
            return jnp.broadcast_to(tab_ref[0, k, pl.ds(i1, 1), :], (8, LANES))

        wave1, lin1, sin1 = one(0), one(1), one(2) * 0.0625
        for h in range(2):
            rows = slice(8 * h, 8 * h + 8)
            wave2 = tab_ref[1, 0, rows, :]
            radius = jnp.sqrt(wave1 * wave1 + wave2 * wave2)
            bend = 0.125 + sin1 * tab_ref[1, 2, rows, :]
            turns = bend * radius + (lin1 + tab_ref[1, 1, rows, :])
            turns = turns - jnp.round(turns)
            cos, sin = cos_sin(turns)
            store(i1, h, cos, sin)


def insert(rest, bit, value):
    low = rest & ((1 << bit) - 1)
    return ((rest >> bit) << (bit + 1)) + (value << bit) + low


def turn_signs():
    row = lax.broadcasted_iota(jnp.int32, (8, LANES), 0)
    return jnp.where(row < 4, -1.0, 1.0).astype(F32)


QUARTERS = ((3, 2), (3, 2), (3, 0), (0, 1))


def quarter_bases(step, quarter):
    slow, fast = QUARTERS[step]
    rest = 6 - step - slow - fast
    base = ((quarter >> 1) << slow) + ((quarter & 1) << fast)
    return (base, base + (1 << rest))


def levels(place, load, cos_of, sin_of, lhs_refs, w_ref, emit, before_level, beside):
    signs = turn_signs()

    def build(step, quarter, lhs_ref):
        for q, base in enumerate(quarter_bases(step, quarter)):
            for r2 in range(8):
                for c in range(4):
                    i1 = base + ((c >> 1) << step)
                    i2 = insert(r2, step, c & 1)
                    value = load(step, place(i1, i2))
                    turned = pltpu.roll(value, 4, 0) * signs
                    for s1 in range(2):
                        parts = []
                        for s2 in range(2):
                            row = (i1 * 4 + (2 * s1 + s2)) * 16 + i2
                            parts.append(value * cos_of(step, row) + turned * sin_of(step, row))
                        both = jnp.concatenate(parts, axis=0)
                        high = both.astype(BF16)
                        low = (both - high.astype(F32)).astype(BF16)
                        start = q * 256 + (r2 * 2 + s1) * 16
                        lhs_ref[start : start + 16, 256 * c : 256 * c + 128] = high
                        lhs_ref[start : start + 16, 256 * c + 128 : 256 * c + 256] = low

    def multiply(step, quarter, lhs_ref):
        y = jnp.dot(lhs_ref[...], w_ref[...], preferred_element_type=F32)
        y = y[:, :LANES] + y[:, LANES:]
        for q, base in enumerate(quarter_bases(step, quarter)):
            for r2 in range(8):
                rows = (q * 8 + r2) * 32
                new = [y[rows + 8 * s : rows + 8 * s + 8] for s in range(4)]
                emit(step, base, r2, new)

    def stage(n):
        if n < 16:
            build(n // 4, n % 4, lhs_refs[n % 2])
        if n > 0:
            multiply((n - 1) // 4, (n - 1) % 4, lhs_refs[(n - 1) % 2])
        if n < 16:
            beside(n // 4, n % 4)

    always = lax.axis_index("sx") >= 0
    for n in range(17):
        if n % 4 == 0 and n < 16:
            before_level(n // 4)
        pl.when(always)(functools.partial(stage, n))


def before_kernel(x_hbm, w_hbm, out_ref, x_ref, w_ref, d0, d1, cos0, sin0, cos1, sin1, tab_ref, lhs0, lhs1, sems):
    copy_x = pltpu.make_async_copy(x_hbm, x_ref, sems.at[0])
    copy_w = pltpu.make_async_copy(w_hbm, w_ref, sems.at[1])
    copy_x.start()
    copy_w.start()
    index_one = lax.axis_index("sx")
    index_two = lax.axis_index("sy")
    lower = lax.broadcasted_iota(jnp.int32, (8, LANES), 1) < RANK
    cos_refs, sin_refs = (cos0, cos1), (sin0, sin1)
    values = (d0, d1)

    def store_in(step):
        def store(i1, s, h, cos, sin):
            cos_refs[step % 2][phase_rows(i1, s, h), :] = cos
            sin_refs[step % 2][phase_rows(i1, s, h), :] = sin

        return store

    for step in range(HALF):
        fill_tables(step, False, index_one, index_two, tab_ref.at[step])

    @pl.loop(0, 16)
    def _(i1):
        phases_at(i1, 0, tab_ref.at[0], store_in(0))

    copy_x.wait()

    @pl.loop(0, 16)
    def _(i1):
        for part in range(2):
            for h in range(2):
                for pair in range(2):
                    cols = slice(pair * LANES, (pair + 1) * LANES)
                    a = x_ref[part, pl.ds(i1, 1), 8 * h : 8 * h + 8, cols].reshape(8, LANES)
                    b = x_ref[part, pl.ds(i1 + 16, 1), 8 * h : 8 * h + 8, cols].reshape(8, LANES)
                    start = (i1 * 16 + 8 * h) * 8 + part * 4 + 2 * pair
                    d0[pl.ds(start, 8, stride=8), :] = jnp.where(lower, a, pltpu.roll(b, RANK, 1))
                    d0[pl.ds(start + 1, 8, stride=8), :] = jnp.where(lower, pltpu.roll(a, RANK, 1), b)

    copy_w.wait()

    def place(i1, i2):
        return i1 * 16 + i2

    def load(step, pos):
        return values[step % 2][pos * 8 : pos * 8 + 8, :]

    def emit(step, base, r2, new):
        if step < HALF - 1:
            for s in range(4):
                pos = place(base + ((s >> 1) << step), insert(r2, step, s & 1))
                values[(step + 1) % 2][pos * 8 : pos * 8 + 8, :] = new[s]
        else:
            for s2 in range(2):
                a, b = new[s2], new[2 + s2]
                row = (base * 16 + insert(r2, step, s2)) * 16
                out_ref[row : row + 8, :] = jnp.where(lower, a, pltpu.roll(b, RANK, 1))
                out_ref[row + 8 : row + 16, :] = jnp.where(lower, pltpu.roll(a, RANK, 1), b)

    def beside(step, quarter):
        if step < HALF - 1:
            for i1 in range(4 * quarter, 4 * quarter + 4):
                phases_at(i1, step + 1, tab_ref.at[step + 1], store_in(step + 1))

    levels(
        place,
        load,
        lambda step, row: cos_refs[step % 2][row : row + 1, :],
        lambda step, row: sin_refs[step % 2][row : row + 1, :],
        (lhs0, lhs1),
        w_ref,
        emit,
        lambda step: None,
        beside,
    )


def phases_kernel(out_ref, tab_ref):
    index_one = lax.axis_index("sx")
    index_two = lax.axis_index("sy")
    for step in range(LEVELS - HALF):

        def store(i1, s, h, cos, sin):
            rows = pl.ds(pl.multiple_of(step * STEP_ROWS + (i1 * 4 + s) * 16 + 8 * h, 8), 8)
            out_ref[0, rows, :] = cos
            out_ref[1, rows, :] = sin

        fill_phases(HALF + step, True, index_one, index_two, tab_ref, store)

    def store_final(i1, h, cos, sin):
        rows = pl.ds(pl.multiple_of((LEVELS - HALF) * STEP_ROWS + i1 * 16 + 8 * h, 8), 8)
        out_ref[0, rows, :] = cos
        out_ref[1, rows, :] = sin

    fill_final(index_one, index_two, tab_ref, store_final)


def after_kernel(x_ref, w_hbm, turns_hbm, out_ref, w_ref, turns_ref, d0, d1, lhs0, lhs1, sems):
    steps = LEVELS - HALF
    copies = []
    for k in range(steps):
        first = k * STEP_ROWS
        rows = pl.ds(first, STEP_ROWS if k < steps - 1 else PHASE_ROWS - first)
        copies.append([pltpu.make_async_copy(turns_hbm.at[:, rows], turns_ref.at[:, rows], sems.at[k])])
    copies[0].append(pltpu.make_async_copy(w_hbm, w_ref, sems.at[steps]))
    for group in copies:
        for copy in group:
            copy.start()
    signs = turn_signs()
    refs = (x_ref, d0, d1, d0, out_ref)

    def place(i1, i2):
        return (i1 >> 1) * 32 + i2 * 2 + (i1 & 1)

    def load(step, pos):
        return refs[step][pos * 8 : pos * 8 + 8, :]

    def emit(step, base, r2, new):
        for s in range(4):
            i1, i2 = base + ((s >> 1) << step), insert(r2, step, s & 1)
            value = new[s]
            if step == steps - 1:
                row = steps * STEP_ROWS + i1 * 16 + i2
                cos, sin = turns_ref[0, row : row + 1, :], turns_ref[1, row : row + 1, :]
                value = value * cos + (pltpu.roll(value, 4, 0) * signs) * sin
            pos = place(i1, i2) * 8
            refs[step + 1][pos : pos + 8, :] = value

    def before_level(step):
        for copy in copies[step]:
            copy.wait()

    levels(
        place,
        load,
        lambda step, row: turns_ref[0, step * STEP_ROWS + row : step * STEP_ROWS + row + 1, :],
        lambda step, row: turns_ref[1, step * STEP_ROWS + row : step * STEP_ROWS + row + 1, :],
        (lhs0, lhs1),
        w_ref,
        emit,
        before_level,
        lambda step, quarter: None,
    )


def order_kernel(x_ref, out_ref):
    lower = lax.broadcasted_iota(jnp.int32, (8, LANES), 1) < RANK
    part = pl.program_id(0)

    @pl.loop(0, 8)
    def _(sx):
        for b4 in range(2):
            for pair in range(2):
                cols = slice(pair * LANES, (pair + 1) * LANES)
                for h in range(2):
                    start = ((sx * 16 + 8 * h) * 2 + b4) * 8 + part * 4 + 2 * pair
                    a = x_ref[pl.ds(start, 8, stride=16), :]
                    b = x_ref[pl.ds(start + 1, 8, stride=16), :]
                    first = jnp.where(lower, a, pltpu.roll(b, RANK, 1))
                    second = jnp.where(lower, pltpu.roll(a, RANK, 1), b)
                    rows = slice(8 * h, 8 * h + 8)
                    out_ref[0, pl.ds(b4 * 16 + sx, 1), rows, cols] = first[None]
                    out_ref[0, pl.ds(b4 * 16 + 8 + sx, 1), rows, cols] = second[None]


VMEM = pl.BlockSpec(memory_space=pltpu.VMEM)
HBM = pl.BlockSpec(memory_space=pltpu.HBM)
ROWS = 2048


def local(weights):
    w = jnp.asarray(mixing_weights())
    shape = jax.ShapeDtypeStruct((ROWS, LANES), F32)
    values = pltpu.VMEM((ROWS, LANES), F32)
    table = pltpu.VMEM((2, 6, 16, LANES), F32)
    lhs = pltpu.VMEM((512, 1024), BF16)
    mixing = pltpu.VMEM((1024, 2 * LANES), BF16)
    cost = functools.partial(pl.CostEstimate, transcendentals=0)

    before = pl.pallas_call(
        before_kernel,
        out_shape=shape,
        in_specs=[HBM, HBM],
        out_specs=VMEM,
        scratch_shapes=[
            pltpu.VMEM(weights.shape, F32),
            mixing,
            values,
            values,
            *[pltpu.VMEM((1024, LANES), F32)] * 4,
            pltpu.VMEM((HALF, 2, 6, 16, LANES), F32),
            lhs,
            lhs,
            pltpu.SemaphoreType.DMA((2,)),
        ],
        compiler_params=pltpu.CompilerParams(vmem_limit_bytes=59 * MIB),
        cost_estimate=cost(flops=4 * 2**31, bytes_accessed=3 * MIB),
        name="before",
    )(weights, w)

    moved = lax.all_to_all(before.reshape(128, 16, LANES), ("sx", "sy"), 0, 0, tiled=True)

    phase = jax.ShapeDtypeStruct((2, PHASE_ROWS, LANES), F32)
    phases = pl.pallas_call(
        phases_kernel,
        out_shape=phase,
        in_specs=[],
        out_specs=VMEM,
        scratch_shapes=[table],
        compiler_params=pltpu.CompilerParams(vmem_limit_bytes=24 * MIB),
        cost_estimate=cost(flops=2**33, bytes_accessed=5 * MIB),
        name="phases",
    )()

    after = pl.pallas_call(
        after_kernel,
        out_shape=shape,
        in_specs=[VMEM, HBM, HBM],
        out_specs=VMEM,
        scratch_shapes=[
            mixing,
            pltpu.VMEM(phase.shape, F32),
            values,
            values,
            lhs,
            lhs,
            pltpu.SemaphoreType.DMA((LEVELS - HALF + 1,)),
        ],
        compiler_params=pltpu.CompilerParams(vmem_limit_bytes=59 * MIB),
        cost_estimate=cost(flops=4 * 2**31, bytes_accessed=8 * MIB),
        name="after",
    )(moved.reshape(ROWS, LANES), w, phases)

    moved = lax.all_to_all(after.reshape(128, 16, LANES), ("sx", "sy"), 0, 0, tiled=True)

    return pl.pallas_call(
        order_kernel,
        out_shape=jax.ShapeDtypeStruct(weights.shape, F32),
        grid=(2,),
        in_specs=[VMEM],
        out_specs=pl.BlockSpec((1, *weights.shape[1:]), lambda part: (part, 0, 0, 0)),
        compiler_params=pltpu.CompilerParams(vmem_limit_bytes=8 * MIB),
        cost_estimate=cost(flops=2**20, bytes_accessed=2 * MIB),
        name="order",
    )(moved.reshape(ROWS, LANES))


def solution(mesh):
    return jax.shard_map(
        local,
        mesh=mesh,
        in_specs=(P(None, "sx", "sy", None),),
        out_specs=P(None, "sx", "sy", None),
        check_vma=False,
    )
```

```python
import functools
import math

import jax
import jax.numpy as jnp
import ml_dtypes
import numpy as np
from jax import lax
from jax.experimental import pallas as pl
from jax.experimental.pallas import tpu as pltpu
from jax.sharding import PartitionSpec as P

CHEB = 8
RANK = 64
GRID = 4096
LEVELS = 8
START = 2
HALF = 4
LANES = 2 * RANK
F32 = jnp.float32
BF16 = jnp.bfloat16
MIB = 1 << 20
STEP_ROWS = 1024
PHASE_ROWS = (LEVELS - HALF) * STEP_ROWS + 256

SIN_TERMS = (6.283184916, -41.34158923, 81.59994333, -76.61447253, 41.34288235, -12.47124353)
COS_TERMS = (0.9999999891, -19.7392045, 64.93911746, -85.45013953, 60.16763095, -25.96759925, 6.528658158)


def lagrange_tables(node_count):
    cheb_nodes = 0.5 * np.cos((2.0 * np.arange(node_count) + 1.0) * math.pi / (2.0 * node_count))
    single = np.ones((2, node_count, node_count))
    for child_bit in range(2):
        for source in range(node_count):
            location = (child_bit - 0.5) / 2.0 + cheb_nodes[source] / 2.0
            for target in range(node_count):
                for another in range(node_count):
                    if another != target:
                        single[child_bit, source, target] *= (location - cheb_nodes[another]) / (
                            cheb_nodes[target] - cheb_nodes[another]
                        )
    paired = single[:, None, :, None, :, None] * single[None, :, None, :, None, :]
    paired = paired.reshape(2, 2, node_count * node_count, node_count * node_count)
    return (cheb_nodes, paired)


def mixing_weights():
    table = lagrange_tables(CHEB)[1].astype(np.float32).reshape(4, RANK, RANK)
    high = table.astype(ml_dtypes.bfloat16)
    low = (table - high.astype(np.float32)).astype(ml_dtypes.bfloat16)
    out = np.zeros((4, 2, LANES, 2, LANES), ml_dtypes.bfloat16)
    for half in range(2):
        part = slice(half * RANK, (half + 1) * RANK)
        for split in range(2):
            out[:, split, part, 0, part] = high
            out[:, split, part, 1, part] = low
    return out.reshape(4 * 2 * LANES, 2 * LANES)


def node_values(lane, dim):
    nodes = lagrange_tables(CHEB)[0].astype(np.float32)
    point = lane & (RANK - 1)
    which = point >> 3 if dim == 0 else point & 7
    out = jnp.full(lane.shape, float(nodes[0]), F32)
    for k in range(1, CHEB):
        out = jnp.where(which == k, float(nodes[k]), out)
    return out


def poly(terms, u):
    acc = terms[-1] * u + terms[-2]
    for term in terms[-3::-1]:
        acc = acc * u + term
    return acc


def sin_turns(f):
    return f * poly(SIN_TERMS, f * f)


def cos_sin(turns):
    f = turns - jnp.round(turns)
    u = f * f
    return poly(COS_TERMS, u), f * poly(SIN_TERMS, u)


def reversed_bits(values, count):
    out = jnp.zeros_like(values)
    for bit in range(count):
        out = out + (((values >> bit) & 1) << (count - 1 - bit))
    return out


def dim_tables(j, after, index, dim):
    row = lax.broadcasted_iota(jnp.int32, (16, LANES), 0)
    lane = lax.broadcasted_iota(jnp.int32, (16, LANES), 1)
    half = (lane >= RANK).astype(jnp.int32)
    if dim == 0:
        g = row * 16 + half * 8 + index if after else index * 32 + half * 16 + row
    else:
        g = row * 16 + index if after else index * 16 + row
    z = node_values(lane, dim)
    b = g >> j
    p = reversed_bits(g & ((1 << j) - 1), j)
    level = START + j
    width = 2.0**level
    wave = (-GRID / 2.0 + (b.astype(F32) + 0.5) * width) + width * z
    odd = ((2 * b + 1) & 7).astype(F32) * 0.125
    linear = odd + 0.25 * z
    p = p.astype(F32)
    parent = sin_turns((p + 0.5) * 0.5**level)
    new = [sin_turns((2.0 * p + (s + 0.5)) * 0.5 ** (level + 1)) for s in range(2)]
    if j == 0:
        lin = []
        for s in range(2):
            whole = (((2 * b + 1) * (2 * s + 1)) & 7).astype(F32) * 0.125
            lin.append(-(whole + ((2 * s + 1) * 0.25) * z))
    else:
        lin = [linear, -linear]
    return wave, lin, parent, new


def store_tables(ref, dim, tables):
    wave, lin, parent, new = tables
    for k, value in enumerate((wave, lin[0], lin[1], parent, new[0], new[1])):
        ref[dim, k] = value


def fill_tables(j, after, index_one, index_two, tab_ref):
    store_tables(tab_ref, 0, dim_tables(j, after, index_one, 0))
    store_tables(tab_ref, 1, dim_tables(j, after, index_two, 1))


def phases_at(i1, j, tab_ref, store):
    def one(k):
        return jnp.broadcast_to(tab_ref[0, k, pl.ds(i1, 1), :], (8, LANES))

    wave1 = one(0)
    wave1 = wave1 * wave1
    lin1 = (one(1), one(2))
    par1, new1 = one(3) * 0.0625, (one(4) * 0.0625, one(5) * 0.0625)
    for h in range(2):

        def two(k):
            return tab_ref[1, k, 8 * h : 8 * h + 8, :]

        wave2 = two(0)
        radius = jnp.sqrt(wave1 + wave2 * wave2)
        lin2 = (two(1), two(2))
        par = par1 * two(3)
        for s1 in range(2):
            for s2 in range(2):
                new = new1[s1] * two(4 + s2)
                bend = -(0.125 + new) if j == 0 else par - new
                turns = bend * radius + (lin1[s1] + lin2[s2])
                cos, sin = cos_sin(turns)
                store(i1, 2 * s1 + s2, h, cos, sin)


def fill_phases(j, after, index_one, index_two, tab_ref, store):
    fill_tables(j, after, index_one, index_two, tab_ref)

    @pl.loop(0, 16)
    def _(i1):
        phases_at(i1, j, tab_ref, store)


def phase_rows(i1, s, h):
    start = (i1 * 4 + s) * 16 + 8 * h
    return pl.ds(start if isinstance(start, int) else pl.multiple_of(start, 8), 8)


def fill_final(index_one, index_two, tab_ref, store):
    row = lax.broadcasted_iota(jnp.int32, (16, LANES), 0)
    lane = lax.broadcasted_iota(jnp.int32, (16, LANES), 1)
    half = (lane >= RANK).astype(jnp.int32)
    for dim in range(2):
        g = row * 16 + half * 8 + index_one if dim == 0 else row * 16 + index_two
        z = node_values(lane, dim)
        p = 2 * reversed_bits(g, LEVELS) + 1
        level = START + LEVELS
        wave = (-GRID / 2.0 + 0.5 * 2.0**level) + 2.0**level * z
        whole = ((-3 * p) & 3).astype(F32) * 0.25
        tab_ref[dim, 0] = wave
        tab_ref[dim, 1] = whole + (p.astype(F32) * 0.5) * z
        tab_ref[dim, 2] = sin_turns(p.astype(F32) * 0.5 ** (level + 1))

    @pl.loop(0, 16)
    def _(i1):
        def one(k):
            return jnp.broadcast_to(tab_ref[0, k, pl.ds(i1, 1), :], (8, LANES))

        wave1, lin1, sin1 = one(0), one(1), one(2) * 0.0625
        for h in range(2):
            rows = slice(8 * h, 8 * h + 8)
            wave2 = tab_ref[1, 0, rows, :]
            radius = jnp.sqrt(wave1 * wave1 + wave2 * wave2)
            bend = 0.125 + sin1 * tab_ref[1, 2, rows, :]
            turns = bend * radius + (lin1 + tab_ref[1, 1, rows, :])
            turns = turns - jnp.round(turns)
            cos, sin = cos_sin(turns)
            store(i1, h, cos, sin)


def insert(rest, bit, value):
    low = rest & ((1 << bit) - 1)
    return ((rest >> bit) << (bit + 1)) + (value << bit) + low


def turn_signs():
    row = lax.broadcasted_iota(jnp.int32, (8, LANES), 0)
    return jnp.where(row < 4, -1.0, 1.0).astype(F32)


QUARTERS = ((3, 2), (3, 2), (3, 0), (0, 1))


def quarter_bases(step, quarter):
    slow, fast = QUARTERS[step]
    rest = 6 - step - slow - fast
    base = ((quarter >> 1) << slow) + ((quarter & 1) << fast)
    return (base, base + (1 << rest))


def levels(place, load, cos_of, sin_of, lhs_refs, w_ref, emit, before_stage, beside):
    signs = turn_signs()

    def build(step, quarter, lhs_ref):
        for q, base in enumerate(quarter_bases(step, quarter)):
            for r2 in range(8):
                for c in range(4):
                    i1 = base + ((c >> 1) << step)
                    i2 = insert(r2, step, c & 1)
                    value = load(step, place(i1, i2))
                    turned = pltpu.roll(value, 4, 0) * signs
                    for s1 in range(2):
                        parts = []
                        for s2 in range(2):
                            row = (i1 * 4 + (2 * s1 + s2)) * 16 + i2
                            parts.append(value * cos_of(step, row) + turned * sin_of(step, row))
                        both = jnp.concatenate(parts, axis=0)
                        high = both.astype(BF16)
                        low = (both - high.astype(F32)).astype(BF16)
                        start = q * 256 + (r2 * 2 + s1) * 16
                        lhs_ref[start : start + 16, 256 * c : 256 * c + 128] = high
                        lhs_ref[start : start + 16, 256 * c + 128 : 256 * c + 256] = low

    def multiply(step, quarter, lhs_ref):
        y = jnp.dot(lhs_ref[...], w_ref[...], preferred_element_type=F32)
        y = y[:, :LANES] + y[:, LANES:]
        for q, base in enumerate(quarter_bases(step, quarter)):
            for r2 in range(8):
                rows = (q * 8 + r2) * 32
                new = [y[rows + 8 * s : rows + 8 * s + 8] for s in range(4)]
                emit(step, base, r2, new)

    def stage(n):
        if n < 16:
            build(n // 4, n % 4, lhs_refs[n % 2])
        if n > 0:
            multiply((n - 1) // 4, (n - 1) % 4, lhs_refs[(n - 1) % 2])
        if n < 16:
            beside(n // 4, n % 4)

    always = lax.axis_index("sx") >= 0
    for n in range(17):
        before_stage(n)
        pl.when(always)(functools.partial(stage, n))


def before_kernel(x_hbm, w_hbm, out_ref, x_ref, w_ref, d0, d1, cos0, sin0, cos1, sin1, tab_ref, lhs0, lhs1, sems):
    copy_x = pltpu.make_async_copy(x_hbm, x_ref, sems.at[0])
    copy_w = pltpu.make_async_copy(w_hbm, w_ref, sems.at[1])
    copy_x.start()
    copy_w.start()
    index_one = lax.axis_index("sx")
    index_two = lax.axis_index("sy")
    lower = lax.broadcasted_iota(jnp.int32, (8, LANES), 1) < RANK
    cos_refs, sin_refs = (cos0, cos1), (sin0, sin1)
    values = (d0, d1)

    def store_in(step):
        def store(i1, s, h, cos, sin):
            cos_refs[step % 2][phase_rows(i1, s, h), :] = cos
            sin_refs[step % 2][phase_rows(i1, s, h), :] = sin

        return store

    for step in range(HALF):
        fill_tables(step, False, index_one, index_two, tab_ref.at[step])

    @pl.loop(0, 16)
    def _(i1):
        phases_at(i1, 0, tab_ref.at[0], store_in(0))

    copy_x.wait()

    @pl.loop(0, 16)
    def _(i1):
        for part in range(2):
            for h in range(2):
                for pair in range(2):
                    cols = slice(pair * LANES, (pair + 1) * LANES)
                    a = x_ref[part, pl.ds(i1, 1), 8 * h : 8 * h + 8, cols].reshape(8, LANES)
                    b = x_ref[part, pl.ds(i1 + 16, 1), 8 * h : 8 * h + 8, cols].reshape(8, LANES)
                    start = (i1 * 16 + 8 * h) * 8 + part * 4 + 2 * pair
                    d0[pl.ds(start, 8, stride=8), :] = jnp.where(lower, a, pltpu.roll(b, RANK, 1))
                    d0[pl.ds(start + 1, 8, stride=8), :] = jnp.where(lower, pltpu.roll(a, RANK, 1), b)

    copy_w.wait()

    def place(i1, i2):
        return i1 * 16 + i2

    def load(step, pos):
        return values[step % 2][pos * 8 : pos * 8 + 8, :]

    def emit(step, base, r2, new):
        if step < HALF - 1:
            for s in range(4):
                pos = place(base + ((s >> 1) << step), insert(r2, step, s & 1))
                values[(step + 1) % 2][pos * 8 : pos * 8 + 8, :] = new[s]
        else:
            for s2 in range(2):
                a, b = new[s2], new[2 + s2]
                row = (base * 16 + insert(r2, step, s2)) * 16
                out_ref[row : row + 8, :] = jnp.where(lower, a, pltpu.roll(b, RANK, 1))
                out_ref[row + 8 : row + 16, :] = jnp.where(lower, pltpu.roll(a, RANK, 1), b)

    def beside(step, quarter):
        if step < HALF - 1:
            for i1 in range(4 * quarter, 4 * quarter + 4):
                phases_at(i1, step + 1, tab_ref.at[step + 1], store_in(step + 1))

    levels(
        place,
        load,
        lambda step, row: cos_refs[step % 2][row : row + 1, :],
        lambda step, row: sin_refs[step % 2][row : row + 1, :],
        (lhs0, lhs1),
        w_ref,
        emit,
        lambda n: None,
        beside,
    )


def phases_kernel(out_ref, tab_ref):
    index_one = lax.axis_index("sx")
    index_two = lax.axis_index("sy")
    for step in range(LEVELS - HALF):

        def store(i1, s, h, cos, sin):
            rows = pl.ds(pl.multiple_of(step * STEP_ROWS + (i1 * 4 + s) * 16 + 8 * h, 8), 8)
            out_ref[0, rows, :] = cos
            out_ref[1, rows, :] = sin

        fill_phases(HALF + step, True, index_one, index_two, tab_ref, store)

    def store_final(i1, h, cos, sin):
        rows = pl.ds(pl.multiple_of((LEVELS - HALF) * STEP_ROWS + i1 * 16 + 8 * h, 8), 8)
        out_ref[0, rows, :] = cos
        out_ref[1, rows, :] = sin

    fill_final(index_one, index_two, tab_ref, store_final)


def after_kernel(x_ref, w_hbm, turns_hbm, out_ref, w_ref, turns_ref, d0, d1, lhs0, lhs1, sems):
    steps = LEVELS - HALF
    quarter = STEP_ROWS // 4
    ends = [0, quarter] + [STEP_ROWS * (k + 1) for k in range(steps - 1)] + [PHASE_ROWS]
    copies = []
    for k in range(steps + 1):
        rows = pl.ds(ends[k], ends[k + 1] - ends[k])
        copies.append(pltpu.make_async_copy(turns_hbm.at[:, rows], turns_ref.at[:, rows], sems.at[k]))
    copy_w = pltpu.make_async_copy(w_hbm, w_ref, sems.at[steps + 1])
    copies[0].start()
    copy_w.start()
    copies[1].start()
    signs = turn_signs()
    refs = (x_ref, d0, d1, d0, out_ref)

    def place(i1, i2):
        return (i1 >> 1) * 32 + i2 * 2 + (i1 & 1)

    def load(step, pos):
        return refs[step][pos * 8 : pos * 8 + 8, :]

    def emit(step, base, r2, new):
        for s in range(4):
            i1, i2 = base + ((s >> 1) << step), insert(r2, step, s & 1)
            value = new[s]
            if step == steps - 1:
                row = steps * STEP_ROWS + i1 * 16 + i2
                cos, sin = turns_ref[0, row : row + 1, :], turns_ref[1, row : row + 1, :]
                value = value * cos + (pltpu.roll(value, 4, 0) * signs) * sin
            pos = place(i1, i2) * 8
            refs[step + 1][pos : pos + 8, :] = value

    def before_stage(n):
        if n == 0:
            copies[0].wait()
            for copy in copies[2:]:
                copy.start()
        if n == 1:
            copy_w.wait()
            copies[1].wait()
        if n in (4, 8, 12):
            copies[1 + n // 4].wait()

    levels(
        place,
        load,
        lambda step, row: turns_ref[0, step * STEP_ROWS + row : step * STEP_ROWS + row + 1, :],
        lambda step, row: turns_ref[1, step * STEP_ROWS + row : step * STEP_ROWS + row + 1, :],
        (lhs0, lhs1),
        w_ref,
        emit,
        before_stage,
        lambda step, quarter: None,
    )


def order_kernel(x_ref, out_ref):
    lower = lax.broadcasted_iota(jnp.int32, (8, LANES), 1) < RANK

    @pl.loop(0, 8)
    def _(sx):
        for b4 in range(2):
            for part in range(2):
                for pair in range(2):
                    cols = slice(pair * LANES, (pair + 1) * LANES)
                    for h in range(2):
                        start = ((sx * 16 + 8 * h) * 2 + b4) * 8 + part * 4 + 2 * pair
                        a = x_ref[pl.ds(start, 8, stride=16), :]
                        b = x_ref[pl.ds(start + 1, 8, stride=16), :]
                        first = jnp.where(lower, a, pltpu.roll(b, RANK, 1))
                        second = jnp.where(lower, pltpu.roll(a, RANK, 1), b)
                        rows = slice(8 * h, 8 * h + 8)
                        out_ref[part, pl.ds(b4 * 16 + sx, 1), rows, cols] = first[None]
                        out_ref[part, pl.ds(b4 * 16 + 8 + sx, 1), rows, cols] = second[None]


VMEM = pl.BlockSpec(memory_space=pltpu.VMEM)
HBM = pl.BlockSpec(memory_space=pltpu.HBM)
ROWS = 2048


def local(weights):
    w = jnp.asarray(mixing_weights())
    shape = jax.ShapeDtypeStruct((ROWS, LANES), F32)
    values = pltpu.VMEM((ROWS, LANES), F32)
    table = pltpu.VMEM((2, 6, 16, LANES), F32)
    lhs = pltpu.VMEM((512, 1024), BF16)
    mixing = pltpu.VMEM((1024, 2 * LANES), BF16)
    cost = functools.partial(pl.CostEstimate, transcendentals=0)

    before = pl.pallas_call(
        before_kernel,
        out_shape=shape,
        in_specs=[HBM, HBM],
        out_specs=VMEM,
        scratch_shapes=[
            pltpu.VMEM(weights.shape, F32),
            mixing,
            values,
            values,
            *[pltpu.VMEM((1024, LANES), F32)] * 4,
            pltpu.VMEM((HALF, 2, 6, 16, LANES), F32),
            lhs,
            lhs,
            pltpu.SemaphoreType.DMA((2,)),
        ],
        compiler_params=pltpu.CompilerParams(vmem_limit_bytes=59 * MIB),
        cost_estimate=cost(flops=4 * 2**31, bytes_accessed=3 * MIB),
        name="before",
    )(weights, w)

    moved = lax.all_to_all(before.reshape(128, 16, LANES), ("sx", "sy"), 0, 0, tiled=True)

    phase = jax.ShapeDtypeStruct((2, PHASE_ROWS, LANES), F32)
    phases = pl.pallas_call(
        phases_kernel,
        out_shape=phase,
        in_specs=[],
        out_specs=VMEM,
        scratch_shapes=[table],
        compiler_params=pltpu.CompilerParams(vmem_limit_bytes=24 * MIB),
        cost_estimate=cost(flops=2**33, bytes_accessed=5 * MIB),
        name="phases",
    )()

    after = pl.pallas_call(
        after_kernel,
        out_shape=shape,
        in_specs=[VMEM, HBM, HBM],
        out_specs=VMEM,
        scratch_shapes=[
            mixing,
            pltpu.VMEM(phase.shape, F32),
            values,
            values,
            lhs,
            lhs,
            pltpu.SemaphoreType.DMA((LEVELS - HALF + 2,)),
        ],
        compiler_params=pltpu.CompilerParams(vmem_limit_bytes=57 * MIB),
        cost_estimate=cost(flops=4 * 2**31, bytes_accessed=8 * MIB),
        name="after",
    )(moved.reshape(ROWS, LANES), w, phases)

    moved = lax.all_to_all(after.reshape(128, 16, LANES), ("sx", "sy"), 0, 0, tiled=True)

    return pl.pallas_call(
        order_kernel,
        out_shape=jax.ShapeDtypeStruct(weights.shape, F32),
        in_specs=[VMEM],
        out_specs=VMEM,
        compiler_params=pltpu.CompilerParams(vmem_limit_bytes=8 * MIB),
        cost_estimate=cost(flops=2**20, bytes_accessed=2 * MIB),
        name="order",
    )(moved.reshape(ROWS, LANES))


def solution(mesh):
    return jax.shard_map(
        local,
        mesh=mesh,
        in_specs=(P(None, "sx", "sy", None),),
        out_specs=P(None, "sx", "sy", None),
        check_vma=False,
    )
```

```python
import functools
import math

import jax
import jax.numpy as jnp
import ml_dtypes
import numpy as np
from jax import lax
from jax.experimental import pallas as pl
from jax.experimental.pallas import tpu as pltpu
from jax.sharding import PartitionSpec as P

CHEB = 8
RANK = 64
GRID = 4096
LEVELS = 8
START = 2
HALF = 4
LANES = 2 * RANK
F32 = jnp.float32
BF16 = jnp.bfloat16
MIB = 1 << 20
STEP_ROWS = 1024
PHASE_ROWS = (LEVELS - HALF) * STEP_ROWS + 256

SIN_TERMS = (6.283184916, -41.34158923, 81.59994333, -76.61447253, 41.34288235, -12.47124353)
COS_TERMS = (0.9999999891, -19.7392045, 64.93911746, -85.45013953, 60.16763095, -25.96759925, 6.528658158)


def lagrange_tables(node_count):
    cheb_nodes = 0.5 * np.cos((2.0 * np.arange(node_count) + 1.0) * math.pi / (2.0 * node_count))
    single = np.ones((2, node_count, node_count))
    for child_bit in range(2):
        for source in range(node_count):
            location = (child_bit - 0.5) / 2.0 + cheb_nodes[source] / 2.0
            for target in range(node_count):
                for another in range(node_count):
                    if another != target:
                        single[child_bit, source, target] *= (location - cheb_nodes[another]) / (
                            cheb_nodes[target] - cheb_nodes[another]
                        )
    paired = single[:, None, :, None, :, None] * single[None, :, None, :, None, :]
    paired = paired.reshape(2, 2, node_count * node_count, node_count * node_count)
    return (cheb_nodes, paired)


def mixing_weights():
    table = lagrange_tables(CHEB)[1].astype(np.float32).reshape(4, RANK, RANK)
    high = table.astype(ml_dtypes.bfloat16)
    low = (table - high.astype(np.float32)).astype(ml_dtypes.bfloat16)
    out = np.zeros((4, 2, LANES, 2, LANES), ml_dtypes.bfloat16)
    for half in range(2):
        part = slice(half * RANK, (half + 1) * RANK)
        for split in range(2):
            out[:, split, part, 0, part] = high
            out[:, split, part, 1, part] = low
    return out.reshape(4 * 2 * LANES, 2 * LANES)


def node_values(lane, dim):
    nodes = lagrange_tables(CHEB)[0].astype(np.float32)
    point = lane & (RANK - 1)
    which = point >> 3 if dim == 0 else point & 7
    out = jnp.full(lane.shape, float(nodes[0]), F32)
    for k in range(1, CHEB):
        out = jnp.where(which == k, float(nodes[k]), out)
    return out


def poly(terms, u):
    acc = terms[-1] * u + terms[-2]
    for term in terms[-3::-1]:
        acc = acc * u + term
    return acc


def sin_turns(f):
    return f * poly(SIN_TERMS, f * f)


def cos_sin(turns):
    f = turns - jnp.round(turns)
    u = f * f
    return poly(COS_TERMS, u), f * poly(SIN_TERMS, u)


def reversed_bits(values, count):
    out = jnp.zeros_like(values)
    for bit in range(count):
        out = out + (((values >> bit) & 1) << (count - 1 - bit))
    return out


def dim_tables(j, after, index, dim):
    row = lax.broadcasted_iota(jnp.int32, (16, LANES), 0)
    lane = lax.broadcasted_iota(jnp.int32, (16, LANES), 1)
    half = (lane >= RANK).astype(jnp.int32)
    if dim == 0:
        g = row * 16 + half * 8 + index if after else index * 32 + half * 16 + row
    else:
        g = row * 16 + index if after else index * 16 + row
    z = node_values(lane, dim)
    b = g >> j
    p = reversed_bits(g & ((1 << j) - 1), j)
    level = START + j
    width = 2.0**level
    wave = (-GRID / 2.0 + (b.astype(F32) + 0.5) * width) + width * z
    odd = ((2 * b + 1) & 7).astype(F32) * 0.125
    linear = odd + 0.25 * z
    p = p.astype(F32)
    parent = sin_turns((p + 0.5) * 0.5**level)
    new = [sin_turns((2.0 * p + (s + 0.5)) * 0.5 ** (level + 1)) for s in range(2)]
    if j == 0:
        lin = []
        for s in range(2):
            whole = (((2 * b + 1) * (2 * s + 1)) & 7).astype(F32) * 0.125
            lin.append(-(whole + ((2 * s + 1) * 0.25) * z))
    else:
        lin = [linear, -linear]
    return wave, lin, parent, new


def store_tables(ref, dim, tables):
    wave, lin, parent, new = tables
    for k, value in enumerate((wave, lin[0], lin[1], parent, new[0], new[1])):
        ref[dim, k] = value


def fill_tables(j, after, index_one, index_two, tab_ref):
    store_tables(tab_ref, 0, dim_tables(j, after, index_one, 0))
    store_tables(tab_ref, 1, dim_tables(j, after, index_two, 1))


def phases_at(i1, j, tab_ref, store):
    def one(k):
        return jnp.broadcast_to(tab_ref[0, k, pl.ds(i1, 1), :], (8, LANES))

    wave1 = one(0)
    wave1 = wave1 * wave1
    lin1 = (one(1), one(2))
    par1, new1 = one(3) * 0.0625, (one(4) * 0.0625, one(5) * 0.0625)
    for h in range(2):

        def two(k):
            return tab_ref[1, k, 8 * h : 8 * h + 8, :]

        wave2 = two(0)
        radius = jnp.sqrt(wave1 + wave2 * wave2)
        lin2 = (two(1), two(2))
        par = par1 * two(3)
        for s1 in range(2):
            for s2 in range(2):
                new = new1[s1] * two(4 + s2)
                bend = -(0.125 + new) if j == 0 else par - new
                turns = bend * radius + (lin1[s1] + lin2[s2])
                cos, sin = cos_sin(turns)
                store(i1, 2 * s1 + s2, h, cos, sin)


def fill_phases(j, after, index_one, index_two, tab_ref, store):
    fill_tables(j, after, index_one, index_two, tab_ref)

    @pl.loop(0, 16)
    def _(i1):
        phases_at(i1, j, tab_ref, store)


def phase_rows(i1, s, h):
    start = (i1 * 4 + s) * 16 + 8 * h
    return pl.ds(start if isinstance(start, int) else pl.multiple_of(start, 8), 8)


def fill_final(index_one, index_two, tab_ref, store):
    row = lax.broadcasted_iota(jnp.int32, (16, LANES), 0)
    lane = lax.broadcasted_iota(jnp.int32, (16, LANES), 1)
    half = (lane >= RANK).astype(jnp.int32)
    for dim in range(2):
        g = row * 16 + half * 8 + index_one if dim == 0 else row * 16 + index_two
        z = node_values(lane, dim)
        p = 2 * reversed_bits(g, LEVELS) + 1
        level = START + LEVELS
        wave = (-GRID / 2.0 + 0.5 * 2.0**level) + 2.0**level * z
        whole = ((-3 * p) & 3).astype(F32) * 0.25
        tab_ref[dim, 0] = wave
        tab_ref[dim, 1] = whole + (p.astype(F32) * 0.5) * z
        tab_ref[dim, 2] = sin_turns(p.astype(F32) * 0.5 ** (level + 1))

    @pl.loop(0, 16)
    def _(i1):
        def one(k):
            return jnp.broadcast_to(tab_ref[0, k, pl.ds(i1, 1), :], (8, LANES))

        wave1, lin1, sin1 = one(0), one(1), one(2) * 0.0625
        for h in range(2):
            rows = slice(8 * h, 8 * h + 8)
            wave2 = tab_ref[1, 0, rows, :]
            radius = jnp.sqrt(wave1 * wave1 + wave2 * wave2)
            bend = 0.125 + sin1 * tab_ref[1, 2, rows, :]
            turns = bend * radius + (lin1 + tab_ref[1, 1, rows, :])
            turns = turns - jnp.round(turns)
            cos, sin = cos_sin(turns)
            store(i1, h, cos, sin)


def insert(rest, bit, value):
    low = rest & ((1 << bit) - 1)
    return ((rest >> bit) << (bit + 1)) + (value << bit) + low


def turn_signs():
    row = lax.broadcasted_iota(jnp.int32, (8, LANES), 0)
    return jnp.where(row < 4, -1.0, 1.0).astype(F32)


QUARTERS = ((3, 2), (3, 2), (3, 0), (0, 1))


def quarter_bases(step, quarter):
    slow, fast = QUARTERS[step]
    rest = 6 - step - slow - fast
    base = ((quarter >> 1) << slow) + ((quarter & 1) << fast)
    return (base, base + (1 << rest))


def levels(place, load, cos_of, sin_of, lhs_refs, w_ref, emit, before_stage, beside):
    signs = turn_signs()

    def build(step, quarter, lhs_ref):
        for q, base in enumerate(quarter_bases(step, quarter)):
            for r2 in range(8):
                for c in range(4):
                    i1 = base + ((c >> 1) << step)
                    i2 = insert(r2, step, c & 1)
                    value = load(step, place(i1, i2))
                    turned = pltpu.roll(value, 4, 0) * signs
                    for s1 in range(2):
                        parts = []
                        for s2 in range(2):
                            row = (i1 * 4 + (2 * s1 + s2)) * 16 + i2
                            parts.append(value * cos_of(step, row) + turned * sin_of(step, row))
                        both = jnp.concatenate(parts, axis=0)
                        high = both.astype(BF16)
                        low = (both - high.astype(F32)).astype(BF16)
                        start = q * 256 + (r2 * 2 + s1) * 16
                        lhs_ref[start : start + 16, 256 * c : 256 * c + 128] = high
                        lhs_ref[start : start + 16, 256 * c + 128 : 256 * c + 256] = low

    def multiply(step, quarter, lhs_ref):
        y = jnp.dot(lhs_ref[...], w_ref[...], preferred_element_type=F32)
        y = y[:, :LANES] + y[:, LANES:]
        for q, base in enumerate(quarter_bases(step, quarter)):
            for r2 in range(8):
                rows = (q * 8 + r2) * 32
                new = [y[rows + 8 * s : rows + 8 * s + 8] for s in range(4)]
                emit(step, base, r2, new)

    def stage(n):
        if n < 16:
            build(n // 4, n % 4, lhs_refs[n % 2])
        if n > 0:
            multiply((n - 1) // 4, (n - 1) % 4, lhs_refs[(n - 1) % 2])
        if n < 16:
            beside(n // 4, n % 4)

    always = lax.axis_index("sx") >= 0
    for n in range(17):
        before_stage(n)
        pl.when(always)(functools.partial(stage, n))


def before_kernel(x_hbm, w_hbm, out_ref, x_ref, w_ref, d0, d1, cos0, sin0, cos1, sin1, tab_ref, lhs0, lhs1, sems):
    copy_x = pltpu.make_async_copy(x_hbm, x_ref, sems.at[0])
    copy_w = pltpu.make_async_copy(w_hbm, w_ref, sems.at[1])
    copy_x.start()
    copy_w.start()
    index_one = lax.axis_index("sx")
    index_two = lax.axis_index("sy")
    lower = lax.broadcasted_iota(jnp.int32, (8, LANES), 1) < RANK
    cos_refs, sin_refs = (cos0, cos1), (sin0, sin1)
    values = (d0, d1)

    def store_in(step):
        def store(i1, s, h, cos, sin):
            cos_refs[step % 2][phase_rows(i1, s, h), :] = cos
            sin_refs[step % 2][phase_rows(i1, s, h), :] = sin

        return store

    for step in range(HALF):
        fill_tables(step, False, index_one, index_two, tab_ref.at[step])

    @pl.loop(0, 16)
    def _(i1):
        phases_at(i1, 0, tab_ref.at[0], store_in(0))

    copy_x.wait()

    @pl.loop(0, 16)
    def _(i1):
        for part in range(2):
            for h in range(2):
                for pair in range(2):
                    cols = slice(pair * LANES, (pair + 1) * LANES)
                    a = x_ref[part, pl.ds(i1, 1), 8 * h : 8 * h + 8, cols].reshape(8, LANES)
                    b = x_ref[part, pl.ds(i1 + 16, 1), 8 * h : 8 * h + 8, cols].reshape(8, LANES)
                    start = (i1 * 16 + 8 * h) * 8 + part * 4 + 2 * pair
                    d0[pl.ds(start, 8, stride=8), :] = jnp.where(lower, a, pltpu.roll(b, RANK, 1))
                    d0[pl.ds(start + 1, 8, stride=8), :] = jnp.where(lower, pltpu.roll(a, RANK, 1), b)

    copy_w.wait()

    def place(i1, i2):
        return i1 * 16 + i2

    def load(step, pos):
        return values[step % 2][pos * 8 : pos * 8 + 8, :]

    def emit(step, base, r2, new):
        if step < HALF - 1:
            for s in range(4):
                pos = place(base + ((s >> 1) << step), insert(r2, step, s & 1))
                values[(step + 1) % 2][pos * 8 : pos * 8 + 8, :] = new[s]
        else:
            for s2 in range(2):
                a, b = new[s2], new[2 + s2]
                row = (base * 16 + insert(r2, step, s2)) * 16
                out_ref[row : row + 8, :] = jnp.where(lower, a, pltpu.roll(b, RANK, 1))
                out_ref[row + 8 : row + 16, :] = jnp.where(lower, pltpu.roll(a, RANK, 1), b)

    def beside(step, quarter):
        if step < HALF - 1:
            for i1 in range(4 * quarter, 4 * quarter + 4):
                phases_at(i1, step + 1, tab_ref.at[step + 1], store_in(step + 1))

    levels(
        place,
        load,
        lambda step, row: cos_refs[step % 2][row : row + 1, :],
        lambda step, row: sin_refs[step % 2][row : row + 1, :],
        (lhs0, lhs1),
        w_ref,
        emit,
        lambda n: None,
        beside,
    )


def phases_kernel(out_ref, tab_ref):
    index_one = lax.axis_index("sx")
    index_two = lax.axis_index("sy")
    for step in range(LEVELS - HALF):

        def store(i1, s, h, cos, sin):
            rows = pl.ds(pl.multiple_of(step * STEP_ROWS + (i1 * 4 + s) * 16 + 8 * h, 8), 8)
            out_ref[0, rows, :] = cos
            out_ref[1, rows, :] = sin

        fill_phases(HALF + step, True, index_one, index_two, tab_ref, store)

    def store_final(i1, h, cos, sin):
        rows = pl.ds(pl.multiple_of((LEVELS - HALF) * STEP_ROWS + i1 * 16 + 8 * h, 8), 8)
        out_ref[0, rows, :] = cos
        out_ref[1, rows, :] = sin

    fill_final(index_one, index_two, tab_ref, store_final)


def after_kernel(x_ref, w_hbm, turns_hbm, out_ref, w_ref, turns_ref, d0, d1, lhs0, lhs1, sems):
    steps = LEVELS - HALF
    quarter = STEP_ROWS // 4
    ends = [0, quarter] + [STEP_ROWS * (k + 1) for k in range(steps - 1)] + [PHASE_ROWS]
    copies = []
    for k in range(steps + 1):
        rows = pl.ds(ends[k], ends[k + 1] - ends[k])
        copies.append(pltpu.make_async_copy(turns_hbm.at[:, rows], turns_ref.at[:, rows], sems.at[k]))
    copy_w = pltpu.make_async_copy(w_hbm, w_ref, sems.at[steps + 1])
    copies[0].start()
    copy_w.start()
    copies[1].start()
    signs = turn_signs()
    refs = (x_ref, d0, d1, d0, out_ref)

    def place(i1, i2):
        return (i1 >> 1) * 32 + i2 * 2 + (i1 & 1)

    def load(step, pos):
        return refs[step][pos * 8 : pos * 8 + 8, :]

    def emit(step, base, r2, new):
        for s in range(4):
            i1, i2 = base + ((s >> 1) << step), insert(r2, step, s & 1)
            value = new[s]
            if step == steps - 1:
                row = steps * STEP_ROWS + i1 * 16 + i2
                cos, sin = turns_ref[0, row : row + 1, :], turns_ref[1, row : row + 1, :]
                value = value * cos + (pltpu.roll(value, 4, 0) * signs) * sin
            pos = place(i1, i2) * 8
            refs[step + 1][pos : pos + 8, :] = value

    def before_stage(n):
        if n == 0:
            copies[0].wait()
            for copy in copies[2:]:
                copy.start()
        if n == 1:
            copy_w.wait()
            copies[1].wait()
        if n in (4, 8, 12):
            copies[1 + n // 4].wait()

    levels(
        place,
        load,
        lambda step, row: turns_ref[0, step * STEP_ROWS + row : step * STEP_ROWS + row + 1, :],
        lambda step, row: turns_ref[1, step * STEP_ROWS + row : step * STEP_ROWS + row + 1, :],
        (lhs0, lhs1),
        w_ref,
        emit,
        before_stage,
        lambda step, quarter: None,
    )


def order_kernel(x_ref, out_ref):
    lower = lax.broadcasted_iota(jnp.int32, (8, LANES), 1) < RANK

    @pl.loop(0, 8)
    def _(sx):
        for b4 in range(2):
            for part in range(2):
                for pair in range(2):
                    cols = slice(pair * LANES, (pair + 1) * LANES)
                    for h in range(2):
                        start = ((sx * 16 + 8 * h) * 2 + b4) * 8 + part * 4 + 2 * pair
                        a = x_ref[pl.ds(start, 8, stride=16), :]
                        b = x_ref[pl.ds(start + 1, 8, stride=16), :]
                        first = jnp.where(lower, a, pltpu.roll(b, RANK, 1))
                        second = jnp.where(lower, pltpu.roll(a, RANK, 1), b)
                        rows = slice(8 * h, 8 * h + 8)
                        out_ref[part, pl.ds(b4 * 16 + sx, 1), rows, cols] = first[None]
                        out_ref[part, pl.ds(b4 * 16 + 8 + sx, 1), rows, cols] = second[None]


VMEM = pl.BlockSpec(memory_space=pltpu.VMEM)
HBM = pl.BlockSpec(memory_space=pltpu.HBM)
ROWS = 2048


def local(weights):
    w = jnp.asarray(mixing_weights())
    shape = jax.ShapeDtypeStruct((ROWS, LANES), F32)
    values = pltpu.VMEM((ROWS, LANES), F32)
    table = pltpu.VMEM((2, 6, 16, LANES), F32)
    lhs = pltpu.VMEM((512, 1024), BF16)
    mixing = pltpu.VMEM((1024, 2 * LANES), BF16)
    cost = functools.partial(pl.CostEstimate, transcendentals=0)

    before = pl.pallas_call(
        before_kernel,
        out_shape=shape,
        in_specs=[HBM, HBM],
        out_specs=VMEM,
        scratch_shapes=[
            pltpu.VMEM(weights.shape, F32),
            mixing,
            values,
            values,
            *[pltpu.VMEM((1024, LANES), F32)] * 4,
            pltpu.VMEM((HALF, 2, 6, 16, LANES), F32),
            lhs,
            lhs,
            pltpu.SemaphoreType.DMA((2,)),
        ],
        compiler_params=pltpu.CompilerParams(vmem_limit_bytes=59 * MIB),
        cost_estimate=cost(flops=4 * 2**31, bytes_accessed=3 * MIB),
        name="before",
    )(weights, w)

    moved = lax.all_to_all(before.reshape(128, 16, LANES), ("sx", "sy"), 0, 0, tiled=True)

    phase = jax.ShapeDtypeStruct((2, PHASE_ROWS, LANES), F32)
    phases = pl.pallas_call(
        phases_kernel,
        out_shape=phase,
        in_specs=[],
        out_specs=VMEM,
        scratch_shapes=[table],
        compiler_params=pltpu.CompilerParams(vmem_limit_bytes=24 * MIB),
        cost_estimate=cost(flops=2**33, bytes_accessed=5 * MIB),
        name="phases",
    )()

    after = pl.pallas_call(
        after_kernel,
        out_shape=shape,
        in_specs=[VMEM, HBM, HBM],
        out_specs=VMEM,
        scratch_shapes=[
            mixing,
            pltpu.VMEM(phase.shape, F32),
            values,
            values,
            lhs,
            lhs,
            pltpu.SemaphoreType.DMA((LEVELS - HALF + 2,)),
        ],
        compiler_params=pltpu.CompilerParams(vmem_limit_bytes=48 * MIB),
        cost_estimate=cost(flops=4 * 2**31, bytes_accessed=8 * MIB),
        name="after",
    )(moved.reshape(ROWS, LANES), w, phases)

    moved = lax.all_to_all(after.reshape(128, 16, LANES), ("sx", "sy"), 0, 0, tiled=True)

    return pl.pallas_call(
        order_kernel,
        out_shape=jax.ShapeDtypeStruct(weights.shape, F32),
        in_specs=[VMEM],
        out_specs=VMEM,
        compiler_params=pltpu.CompilerParams(vmem_limit_bytes=8 * MIB),
        cost_estimate=cost(flops=2**20, bytes_accessed=2 * MIB),
        name="order",
    )(moved.reshape(ROWS, LANES))


def solution(mesh):
    return jax.shard_map(
        local,
        mesh=mesh,
        in_specs=(P(None, "sx", "sy", None),),
        out_specs=P(None, "sx", "sy", None),
        check_vma=False,
    )
```
